128 devices in a mesh: tm: 16 (over x, z), rows: 8 (over y, core).
Axes of the slice: x: 4, y: 4, z: 4, core: 2. Of those that a mesh axis runs over, the one named last changes fastest.
Arguments:
- tile_values: bfloat16 [65536, 128, 128], P(('tm', 'rows')), may hold values from -6 to 6
- tile_users: int32 [65536], P(('tm', 'rows')), may hold values from 0 to 127
- tile_items: int32 [65536], P(('tm', 'rows')), may hold values from 0 to 127
- tile_steps: int32 [65536], P(('tm', 'rows')), may hold values from 0 to 7
- tile_count: int32 [128], P(('tm', 'rows')), may hold values from 64 to 512, as said below
- users_ask: int32 [16384, 1], P(('tm', 'rows')), may hold values from 0 to 7, as said below
- items_ask: int32 [16384, 1], P(('tm', 'rows')), may hold values from 0 to 7, as said below
- user_factor: float32 [1024, 64, 128], P(('tm', 'rows')), may hold values from -6 to 6
- item_factor: float32 [1024, 64, 128], P(('tm', 'rows')), may hold values from -6 to 6
- time_factor: float32 [128, 64], P('tm'), may hold values from -2 to 2
- core: float32 [64, 64, 64], replicated, may hold values from -0.25 to 0.25
Outputs:
- grad_users: float32 [1024, 64, 128], P(('tm', 'rows'))
- grad_items: float32 [1024, 64, 128], P(('tm', 'rows'))
- grad_time: float32 [128, 64], P('tm')
- grad_core: float32 [64, 64, 64], replicated
The draws below stay inside these ranges and needn't reach their ends.
Inputs may be any that keep to these rules, and one draw needn't show every extreme that they name: `users_ask`: each row holds 1 distinct local block numbers of the owner that the row names. `items_ask`: each row holds 1 distinct local block numbers of the owner that the row names. `tile_count`: slots of a device at or past its count are padding; some device is full.
All inputs are finite; a program needn't handle non-finite values.
Results may differ from the reference program's by a relative error of at most 0.0003.
Values sent between devices are 32-bit elements; how exact they have to be, the bound alone decides.
No kernel may reach another device: no remote copies, remote signals or barrier semaphores. Data moves between devices by JAX's collectives and lax.ppermute only.
A program may use at most 128 MiB of HBM per device.

```python
import jax
import jax.numpy as jnp
from jax import lax

RANK = 64
BLOCK = 128
TILE_DEV = 512
BLOCKS_DEV = 8
STEP_DEV = 8
CAP = 1
OWNERS = 128
NB = 1024
TILES = 65536
STEPS = 128
N_ROWS = 8


def pick_rows(key):
    row_keys = jax.random.split(key, OWNERS * OWNERS)

    def pick_one(row_key):
        return jax.random.permutation(row_key, BLOCKS_DEV)[:CAP]
    return jax.vmap(pick_one)(row_keys).astype(jnp.int32)


def draw_users_ask(key, part):
    key = jax.random.fold_in(key, 1)
    return pick_rows(key)


def draw_items_ask(key, part):
    key = jax.random.fold_in(key, 2)
    return pick_rows(key)


def draw_tile_count(key, part):
    key = jax.random.fold_in(key, 3)
    powers = jax.random.randint(key, (OWNERS,), 0, 4)
    counts = TILE_DEV // jnp.left_shift(jnp.ones((OWNERS,), jnp.int32), powers.astype(jnp.int32))
    fullest = jax.random.randint(jax.random.fold_in(key, 7), (), 0, OWNERS)
    return counts.at[fullest].set(TILE_DEV).astype(jnp.int32)


def with_ends(drawn, own_key, smallest, largest):
    place = [jax.random.randint(jax.random.fold_in(own_key, axis), (), 0, length) for axis, length in enumerate(drawn.shape)]
    longest = drawn.shape.index(max(drawn.shape))
    next_to = place[:longest] + [(place[longest] + 1) % drawn.shape[longest]] + place[longest + 1:]
    return drawn.at[tuple(place)].set(smallest).at[tuple(next_to)].set(largest)


def shard_levels(rng, extent, cuts, least, largest):
    level, own = 1.0, jax.random.fold_in(rng, 6)
    for axis_at, shards_of in cuts:
        heights = jnp.exp(jax.random.uniform(jax.random.fold_in(own, axis_at), (shards_of,), jnp.float32, least / len(cuts), largest / len(cuts)))
        level = level * jnp.repeat(heights, extent[axis_at] // shards_of).reshape([-1 if axis == axis_at else 1 for axis in range(len(extent))])
    return level


def gaussian(own_key, dims, deviation, most, shards=(), kind=jnp.bfloat16):
    entries = deviation * jax.random.normal(own_key, dims, jnp.float32)
    if shards:
        entries = entries * shard_levels(own_key, dims, shards, -0.22, 0.18)
    return jnp.clip(entries, -most, most).astype(kind)


def setup_inputs(seed: int = 0) -> dict:
    key_of = jax.random.split(jax.random.key(seed), 12)
    return {
        "tile_values": gaussian(key_of[0], (TILES, BLOCK, BLOCK), 1.0, 6.0, ((0, 128),)),
        "tile_users": with_ends(jax.random.randint(key_of[1], (TILES,), 0, OWNERS * CAP), jax.random.fold_in(key_of[1], 1), 0, (OWNERS * CAP) - 1).astype(jnp.int32),
        "tile_items": with_ends(jax.random.randint(key_of[2], (TILES,), 0, OWNERS * CAP), jax.random.fold_in(key_of[2], 1), 0, (OWNERS * CAP) - 1).astype(jnp.int32),
        "tile_steps": with_ends(jax.random.randint(key_of[3], (TILES,), 0, STEP_DEV), jax.random.fold_in(key_of[3], 1), 0, STEP_DEV - 1).astype(jnp.int32),
        "tile_count": draw_tile_count(jax.random.fold_in(key_of[11], 71), 0),
        "users_ask": draw_users_ask(jax.random.fold_in(key_of[11], 71), 0),
        "items_ask": draw_items_ask(jax.random.fold_in(key_of[11], 71), 0),
        "user_factor": gaussian(key_of[7], (NB, RANK, BLOCK), 1.0, 6.0, ((0, 128),), jnp.float32),
        "item_factor": gaussian(key_of[8], (NB, RANK, BLOCK), 1.0, 6.0, ((0, 128),), jnp.float32),
        "time_factor": gaussian(key_of[9], (STEPS, RANK), (RANK ** -0.5), 2.0, ((0, 16),), jnp.float32),
        "core": gaussian(key_of[10], (RANK, RANK, RANK), (1.0 / RANK), 0.25, (), jnp.float32),
    }


HIGH = lax.Precision.HIGHEST
user_scale = 0.125
time_scale = 1.0 / 2048.0
core_scale = 1.0 / 4096.0


def reference(tile_values, tile_users, tile_items, tile_steps, tile_count, users_ask, items_ask, user_factor, item_factor, time_factor, core):
    asks_user = users_ask.reshape(OWNERS, OWNERS * CAP)
    asks_item = items_ask.reshape(OWNERS, OWNERS * CAP)

    def visit(carry, device):
        grad_left, grad_right, step_sums = carry
        start = device * TILE_DEV
        values = lax.dynamic_slice_in_dim(tile_values, start, TILE_DEV, 0).astype(jnp.float32)
        slots_user = lax.dynamic_slice_in_dim(tile_users, start, TILE_DEV, 0)
        slots_item = lax.dynamic_slice_in_dim(tile_items, start, TILE_DEV, 0)
        local_steps = lax.dynamic_slice_in_dim(tile_steps, start, TILE_DEV, 0)
        ids_user = ((slots_user // CAP) * BLOCKS_DEV + asks_user[device][slots_user]).astype(jnp.int32)
        ids_item = ((slots_item // CAP) * BLOCKS_DEV + asks_item[device][slots_item]).astype(jnp.int32)
        steps = ((device // N_ROWS) * STEP_DEV + local_steps).astype(jnp.int32)
        left = user_factor[ids_user]
        right = item_factor[ids_item]
        cores = jnp.einsum('pqr,tr->tpq', core, time_factor[steps], precision=HIGH)
        live = (jnp.arange(TILE_DEV, dtype=jnp.int32) < tile_count[device]).astype(jnp.float32)
        mixed = jnp.einsum('tpq,tqj->tpj', cores, right, precision=HIGH)
        guess = jnp.einsum('tpi,tpj->tij', left, mixed, precision=HIGH)
        resid = (guess - values) * live[:, None, None]
        grad_u = jnp.einsum('tij,tpj->tpi', resid, mixed, precision=HIGH)
        across = jnp.einsum('tpi,tpq->tqi', left, cores, precision=HIGH)
        grad_v = jnp.einsum('tij,tqi->tqj', resid, across, precision=HIGH)
        inner = jnp.einsum('tpi,tij->tpj', left, resid, precision=HIGH)
        dcore = jnp.einsum('tpj,tqj->tpq', inner, right, precision=HIGH)
        grad_left = grad_left.at[ids_user].add(grad_u)
        grad_right = grad_right.at[ids_item].add(grad_v)
        step_sums = step_sums.at[steps].add(dcore)
        return (grad_left, grad_right, step_sums), None

    start_carry = (jnp.zeros((NB, RANK, BLOCK), jnp.float32), jnp.zeros((NB, RANK, BLOCK), jnp.float32), jnp.zeros((STEPS, RANK, RANK), jnp.float32))
    (grad_left, grad_right, step_sums), unused = lax.scan(visit, start_carry, jnp.arange(OWNERS, dtype=jnp.int32))
    grad_time = time_scale * jnp.einsum('spq,pqr->sr', step_sums, core, precision=HIGH)
    grad_core = core_scale * jnp.einsum('spq,sr->pqr', step_sums, time_factor, precision=HIGH)
    return (user_scale * grad_left, user_scale * grad_right, grad_time, grad_core)
```

```python
import functools

import jax
import jax.numpy as jnp
from jax import lax
from jax.experimental import pallas as pl
from jax.experimental.pallas import tpu as pltpu
from jax.sharding import PartitionSpec as P

HIGH = lax.Precision.HIGHEST
user_scale = 0.125
time_scale = 1.0 / 2048.0
core_scale = 1.0 / 4096.0

BF = jnp.bfloat16
F32 = jnp.float32
AXES = ("tm", "rows")
cat = jnp.concatenate


def split(x):
    hi = x.astype(BF)
    lo = (x - hi.astype(F32)).astype(BF)
    return hi, lo


def mul(a, b):
    return lax.dot_general(a, b, (((1,), (0,)), ((), ())), preferred_element_type=F32)


def mul_t(a, b):
    return lax.dot_general(a, b, (((1,), (1,)), ((), ())), preferred_element_type=F32)


def tiles_kernel(
    group, slots_user, slots_item, steps, count,
    values, users, items, cores,
    grad_left, grad_right, sums,
    left_t, left, right, core_hl, core_t,
):
    rank = users.shape[1]
    width = users.shape[2]
    block = pl.program_id(0)
    live_count = count[0]

    @pl.when(block == 0)
    def _():
        grad_left[...] = jnp.zeros_like(grad_left)
        grad_right[...] = jnp.zeros_like(grad_right)
        sums[...] = jnp.zeros_like(sums)

        def prep(k, carry):
            x = users[k]
            left[k] = cat(split(x), 0)
            left_t[k] = cat(split(x.T), 1)
            right[k] = cat(split(items[k]), 0)
            return carry

        lax.fori_loop(0, users.shape[0], prep, 0, unroll=4)

        def prep_core(k, carry):
            x = cores[k]
            core_hl[k] = cat(split(x), 1)
            core_t[k] = cat(split(x.T), 1)
            return carry

        lax.fori_loop(0, cores.shape[0], prep_core, 0)

    @pl.when(block * group < live_count)
    def _():
        span = range(group)
        tile = [block * group + t for t in span]
        user = [slots_user[k] for k in tile]
        item = [slots_item[k] for k in tile]
        step = [steps[k] for k in tile]
        rights = [right[v] for v in item]
        mixed = []
        for t in span:
            hi, lo = rights[t][:rank], rights[t][rank:]
            c = core_hl[step[t]]
            mixed.append(mul(cat([c, c], 1), cat([hi, hi, lo, lo], 0)))
        mixed = [split(m) for m in mixed]
        guess = []
        for t in span:
            hi, lo = mixed[t]
            x = left_t[user[t]]
            guess.append(mul(cat([x, x], 1), cat([hi, hi, lo, lo], 0)))
        resid = [
            split(jnp.where(tile[t] < live_count, guess[t] - values[t].astype(F32), 0.0))
            for t in span
        ]
        inner = []
        for t in span:
            a = mul(left[user[t]], cat(resid[t], 1))
            inner.append((a[:rank, :width] + a[:rank, width:]) + (a[rank:, :width] + a[rank:, width:]))
        grad_u = []
        for t in span:
            a = mul_t(cat(mixed[t], 0), cat(resid[t], 0))
            grad_u.append((a[:rank, :width] + a[:rank, width:]) + (a[rank:, :width] + a[rank:, width:]))
        inner = [split(x) for x in inner]
        grad_v = []
        for t in span:
            hi, lo = inner[t]
            c = core_t[step[t]]
            grad_v.append(mul(cat([c, c], 1), cat([hi, hi, lo, lo], 0)))
        dcore = []
        for t in span:
            a = mul_t(cat(inner[t], 0), rights[t])
            a = a[:rank] + a[rank:]
            dcore.append(a[:, :rank] + a[:, rank:])
        for t in span:
            grad_left[user[t]] += grad_u[t]
            grad_right[item[t]] += grad_v[t]
            sums[step[t]] += dcore[t]


def tiles_call(slots_user, slots_item, steps, count, values, users, items, cores):
    group = 16
    slots, width = values.shape[0], values.shape[1]
    rank = users.shape[1]

    def whole(shape):
        return pl.BlockSpec(shape, lambda b, *_: (0,) * len(shape), pipeline_mode=pl.Buffered(1))

    def values_at(b, su, si, st, cnt):
        last = jnp.maximum((cnt[0] + group - 1) // group - 1, 0)
        return (jnp.minimum(b, last), 0, 0)

    return pl.pallas_call(
        functools.partial(tiles_kernel, group),
        grid_spec=pltpu.PrefetchScalarGridSpec(
            num_scalar_prefetch=4,
            grid=(slots // group,),
            in_specs=[
                pl.BlockSpec((group, width, width), values_at),
                whole(users.shape),
                whole(items.shape),
                whole(cores.shape),
            ],
            out_specs=[whole(users.shape), whole(items.shape), whole(cores.shape)],
            scratch_shapes=[
                pltpu.VMEM((users.shape[0], width, 2 * rank), BF),
                pltpu.VMEM((users.shape[0], 2 * rank, width), BF),
                pltpu.VMEM((items.shape[0], 2 * rank, width), BF),
                pltpu.VMEM((cores.shape[0], rank, 2 * rank), BF),
                pltpu.VMEM((cores.shape[0], rank, 2 * rank), BF),
            ],
        ),
        out_shape=[
            jax.ShapeDtypeStruct(users.shape, F32),
            jax.ShapeDtypeStruct(items.shape, F32),
            jax.ShapeDtypeStruct(cores.shape, F32),
        ],
        compiler_params=pltpu.CompilerParams(
            vmem_limit_bytes=60 * 2**20, dimension_semantics=("arbitrary",)
        ),
        name="tiles",
    )(slots_user, slots_item, steps, count, values, users, items, cores)


def owner_kernel(group, held, back, out):
    block = pl.program_id(0)

    @pl.when(block == 0)
    def _():
        out[...] = jnp.zeros_like(out)

    for t in range(group):
        out[held[block * group + t]] += back[t]

    @pl.when(block == pl.num_programs(0) - 1)
    def _():
        out[...] = out[...] * user_scale


def owner_sum(held, back, blocks_own):
    group = 16
    total, rank, width = back.shape
    return pl.pallas_call(
        functools.partial(owner_kernel, group),
        grid_spec=pltpu.PrefetchScalarGridSpec(
            num_scalar_prefetch=1,
            grid=(total // group,),
            in_specs=[pl.BlockSpec((group, rank, width), lambda b, *_: (b, 0, 0))],
            out_specs=pl.BlockSpec((blocks_own, rank, width), lambda b, *_: (0, 0, 0)),
        ),
        out_shape=jax.ShapeDtypeStruct((blocks_own, rank, width), F32),
        compiler_params=pltpu.CompilerParams(dimension_semantics=("arbitrary",)),
        name="owners",
    )(held, back)


def to_all(x):
    return lax.all_to_all(x, AXES, split_axis=0, concat_axis=0, tiled=True)


def shards(
    tile_values,
    tile_users,
    tile_items,
    tile_steps,
    tile_count,
    users_ask,
    items_ask,
    user_factor,
    item_factor,
    time_factor,
    core,
):
    rank = user_factor.shape[1]
    width = user_factor.shape[2]
    blocks_own = user_factor.shape[0]
    step_count = time_factor.shape[0]
    asks = to_all(cat([users_ask, items_ask], 1))
    held_user, held_item = asks[:, 0], asks[:, 1]
    found_user = user_factor.at[held_user].get(mode="promise_in_bounds")
    found_item = item_factor.at[held_item].get(mode="promise_in_bounds")
    users = to_all(found_user)
    items = to_all(found_item)
    step_cores = jnp.einsum("pqr,sr->spq", core, time_factor, precision=HIGH)
    slot_left, slot_right, step_sums = tiles_call(
        tile_users, tile_items, tile_steps, tile_count, tile_values, users, items, step_cores
    )
    mine = lax.all_to_all(
        step_sums.reshape(step_count, rank * rank), "rows", split_axis=0, concat_axis=0, tiled=True
    )
    total = jnp.sum(mine, axis=0)
    every_time = lax.all_gather(time_factor, "tm", axis=0, tiled=True)
    every = lax.all_gather(total, AXES, axis=0, tiled=False)
    slice_at = lax.axis_index("tm") * step_count
    own = lax.dynamic_slice_in_dim(every, slice_at, step_count, 0)
    grad_time = time_scale * jnp.einsum(
        "sk,kr->sr", own, core.reshape(rank * rank, rank), precision=HIGH
    )
    grad_core = core_scale * jnp.einsum("sk,sr->kr", every, every_time, precision=HIGH)
    grad_core = grad_core.reshape(rank, rank, rank)
    back_left = to_all(slot_left)
    back_right = to_all(slot_right)
    grad_users = owner_sum(held_user, back_left, blocks_own)
    grad_items = owner_sum(held_item, back_right, blocks_own)
    return (grad_users, grad_items, grad_time, grad_core)


def solution(mesh):
    in_specs = (
        P(AXES, None, None),
        P(AXES),
        P(AXES),
        P(AXES),
        P(AXES),
        P(AXES, None),
        P(AXES, None),
        P(AXES, None, None),
        P(AXES, None, None),
        P("tm", None),
        P(),
    )
    out_specs = (P(AXES, None, None), P(AXES, None, None), P("tm", None), P())
    return jax.shard_map(shards, mesh=mesh, in_specs=in_specs, out_specs=out_specs, check_vma=False)
```

```python
import functools

import jax
import jax.numpy as jnp
from jax import lax
from jax.experimental import pallas as pl
from jax.experimental.pallas import tpu as pltpu
from jax.sharding import PartitionSpec as P

HIGH = lax.Precision.HIGHEST
user_scale = 0.125
time_scale = 1.0 / 2048.0
core_scale = 1.0 / 4096.0

BF = jnp.bfloat16
F32 = jnp.float32
AXES = ("tm", "rows")
cat = jnp.concatenate
PREP = 8


def split(x):
    hi = x.astype(BF)
    lo = (x - hi.astype(F32)).astype(BF)
    return hi, lo


def mul(a, b):
    return lax.dot_general(a, b, (((1,), (0,)), ((), ())), preferred_element_type=F32)


def mul_t(a, b):
    return lax.dot_general(a, b, (((1,), (1,)), ((), ())), preferred_element_type=F32)


def twice(x):
    return cat([x, x], 1)


def quad(hi, lo):
    return cat([hi, hi, lo, lo], 0)


def pairs(hi, lo):
    return cat([twice(hi), twice(lo)], 0)


def whole(shape):
    return pl.BlockSpec(shape, lambda b, *_: (0,) * len(shape), pipeline_mode=pl.Buffered(1))


def live_block(group):
    def at(b, *scalars):
        last = jnp.maximum((scalars[-1][0] + group - 1) // group - 1, 0)
        return (jnp.minimum(b, last), 0, 0)
    return at


def params():
    return pltpu.CompilerParams(vmem_limit_bytes=60 * 2**20, dimension_semantics=("arbitrary",))


def in_groups(total, size, step):
    def one(g, carry):
        step([g * size + t for t in range(size)])
        return carry
    lax.fori_loop(0, total // size, one, 0)


def item_kernel(group, slots_user, slots_item, steps, count, items, cores, values,
                gram, moved, mixed_out, right, core_hl, gram_sum):
    rank, width = items.shape[1], items.shape[2]
    block = pl.program_id(0)

    @pl.when(block == 0)
    def _():
        def prep(ks):
            out = [cat(split(items[k]), 0) for k in ks]
            for k, x in zip(ks, out):
                right[k] = x
            for k in ks:
                gram_sum[k] = jnp.zeros_like(gram_sum[k])
                moved[k] = jnp.zeros_like(moved[k])
        in_groups(items.shape[0], PREP, prep)
        for k in range(cores.shape[0]):
            core_hl[k] = cat(split(cores[k]), 1)

    @pl.when(block * group < count[0])
    def _():
        span = range(group)
        tile = [block * group + t for t in span]
        user = [slots_user[k] for k in tile]
        mixed = []
        for t in span:
            r = right[slots_item[tile[t]]]
            mixed.append(mul(twice(core_hl[steps[tile[t]]]), quad(r[:rank], r[rank:])))
        mixed = [split(jnp.where(tile[t] < count[0], mixed[t], 0.0)) for t in span]
        both = []
        for t in span:
            v = values[t]
            both.append(mul_t(cat(mixed[t], 1), cat([twice(v), pairs(*mixed[t])], 0)))
        for t in span:
            mixed_out[t] = cat(mixed[t], 0)
        for t in span:
            moved[user[t]] += both[t][:, :width]
            gram_sum[user[t]] += both[t][:, width:]

    @pl.when(block == pl.num_programs(0) - 1)
    def _():
        def finish(ks):
            out = [gram_sum[k] for k in ks]
            out = [cat(split(x[:, :rank] + x[:, rank:]), 1) for x in out]
            for k, x in zip(ks, out):
                gram[k] = x
        in_groups(gram.shape[0], PREP, finish)


def item_call(slots_user, slots_item, steps, count, items, cores, values, group=32):
    slots, width = values.shape[:2]
    held, rank = items.shape[:2]
    return pl.pallas_call(
        functools.partial(item_kernel, group),
        grid_spec=pltpu.PrefetchScalarGridSpec(
            num_scalar_prefetch=4,
            grid=(slots // group,),
            in_specs=[whole(items.shape), whole(cores.shape),
                      pl.BlockSpec((group, width, width), live_block(group))],
            out_specs=[whole((held, rank, 2 * rank)), whole((held, rank, width)),
                       pl.BlockSpec((group, 2 * rank, width), live_block(group)),
                       whole((held, 2 * rank, width))],
            scratch_shapes=[pltpu.VMEM((cores.shape[0], rank, 2 * rank), BF),
                            pltpu.VMEM((held, rank, 2 * rank), F32)],
        ),
        out_shape=[jax.ShapeDtypeStruct((held, rank, 2 * rank), BF),
                   jax.ShapeDtypeStruct((held, rank, width), F32),
                   jax.ShapeDtypeStruct((slots, 2 * rank, width), BF),
                   jax.ShapeDtypeStruct((held, 2 * rank, width), BF)],
        compiler_params=params(),
        cost_estimate=pl.CostEstimate(flops=2 * 10**10, bytes_accessed=5 * 10**7, transcendentals=0),
        name="item_side",
    )(slots_user, slots_item, steps, count, items, cores, values)


def user_grad_kernel(group, users, gram, moved, grad):
    span = range(group)
    out = [mul(twice(gram[t]), quad(*split(users[t]))) for t in span]
    for t in span:
        grad[t] = out[t] - moved[t]


def user_grad_call(users, gram, moved, group=16):
    held, rank, width = users.shape
    block = pl.BlockSpec((group, rank, width), lambda b: (b, 0, 0))
    return pl.pallas_call(
        functools.partial(user_grad_kernel, group),
        grid=(held // group,),
        in_specs=[block, pl.BlockSpec((group, rank, 2 * rank), lambda b: (b, 0, 0)), block],
        out_specs=block,
        out_shape=jax.ShapeDtypeStruct(users.shape, F32),
        compiler_params=params(),
        cost_estimate=pl.CostEstimate(flops=10**9, bytes_accessed=2 * 10**7, transcendentals=0),
        name="user_grad",
    )(users, gram, moved)


def tile_kernel(group, slots_user, slots_item, steps, count, users, right, cores, values, mixed,
                grad, sums, left, core_t, sums_hl):
    rank, width = users.shape[1], users.shape[2]
    block = pl.program_id(0)

    @pl.when(block == 0)
    def _():
        def prep(ks):
            x = [split(users[k]) for k in ks]
            h = [mul_t(cat(y, 1), pairs(*y)) for y in x]
            h = [cat(split(y[:, :rank] + y[:, rank:]), 1) for y in h]
            for k, y, z in zip(ks, x, h):
                left[k] = cat([-y[0], -y[1], z], 1)
                grad[k] = jnp.zeros_like(grad[k])
        in_groups(users.shape[0], PREP, prep)
        for k in range(cores.shape[0]):
            core_t[k] = cat(split(cores[k].T), 1)
        sums_hl[...] = jnp.zeros_like(sums_hl)

    @pl.when(block * group < count[0])
    def _():
        span = range(group)
        tile = [block * group + t for t in span]
        item = [slots_item[k] for k in tile]
        step = [steps[k] for k in tile]
        inner = []
        for t in span:
            x = left[slots_user[tile[t]]]
            v, m = values[t], mixed[t]
            inner.append(mul(cat([x, x[:, 2 * width:]], 1), cat([v, v, quad(m[:rank], m[rank:])], 0)))
        inner = [split(jnp.where(tile[t] < count[0], inner[t], 0.0)) for t in span]
        grad_v = [mul(twice(core_t[step[t]]), quad(*inner[t])) for t in span]
        dcore = []
        for t in span:
            a = mul_t(cat(inner[t], 0), right[item[t]])
            dcore.append(a[:rank] + a[rank:])
        for t in span:
            grad[item[t]] += grad_v[t]
            sums_hl[step[t]] += dcore[t]

    @pl.when(block == pl.num_programs(0) - 1)
    def _():
        for k in range(sums.shape[0]):
            a = sums_hl[k]
            sums[k] = a[:, :rank] + a[:, rank:]


def tile_call(slots_user, slots_item, steps, count, users, right, cores, values, mixed, group=32):
    slots, width = values.shape[:2]
    held, rank = users.shape[:2]
    return pl.pallas_call(
        functools.partial(tile_kernel, group),
        grid_spec=pltpu.PrefetchScalarGridSpec(
            num_scalar_prefetch=4,
            grid=(slots // group,),
            in_specs=[whole(users.shape), whole(right.shape), whole(cores.shape),
                      pl.BlockSpec((group, width, width), live_block(group)),
                      pl.BlockSpec((group, 2 * rank, width), live_block(group))],
            out_specs=[whole((held, rank, width)), whole(cores.shape)],
            scratch_shapes=[pltpu.VMEM((held, rank, 2 * width + 2 * rank), BF),
                            pltpu.VMEM((cores.shape[0], rank, 2 * rank), BF),
                            pltpu.VMEM((cores.shape[0], rank, 2 * rank), F32)],
        ),
        out_shape=[jax.ShapeDtypeStruct((held, rank, width), F32),
                   jax.ShapeDtypeStruct(cores.shape, F32)],
        compiler_params=params(),
        cost_estimate=pl.CostEstimate(flops=3 * 10**10, bytes_accessed=5 * 10**7, transcendentals=0),
        name="tile_side",
    )(slots_user, slots_item, steps, count, users, right, cores, values, mixed)

def owner_kernel(group, held, back, out):
    block = pl.program_id(0)

    @pl.when(block == 0)
    def _():
        out[...] = jnp.zeros_like(out)

    for t in range(group):
        out[held[block * group + t]] += back[t]

    @pl.when(block == pl.num_programs(0) - 1)
    def _():
        out[...] = out[...] * user_scale


def owner_sum(held, back, blocks_own):
    group = 16
    total, rank, width = back.shape
    return pl.pallas_call(
        functools.partial(owner_kernel, group),
        grid_spec=pltpu.PrefetchScalarGridSpec(
            num_scalar_prefetch=1,
            grid=(total // group,),
            in_specs=[pl.BlockSpec((group, rank, width), lambda b, *_: (b, 0, 0))],
            out_specs=pl.BlockSpec((blocks_own, rank, width), lambda b, *_: (0, 0, 0)),
        ),
        out_shape=jax.ShapeDtypeStruct((blocks_own, rank, width), F32),
        compiler_params=pltpu.CompilerParams(dimension_semantics=("arbitrary",)),
        name="owners",
    )(held, back)


def to_all(x):
    return lax.all_to_all(x, AXES, split_axis=0, concat_axis=0, tiled=True)


def shards(
    tile_values,
    tile_users,
    tile_items,
    tile_steps,
    tile_count,
    users_ask,
    items_ask,
    user_factor,
    item_factor,
    time_factor,
    core,
):
    rank = user_factor.shape[1]
    width = user_factor.shape[2]
    blocks_own = user_factor.shape[0]
    step_count = time_factor.shape[0]
    count_tm = lax.axis_size("tm")
    count_rows = lax.axis_size("rows")
    owners = count_tm * count_rows
    asks = to_all(cat([users_ask, items_ask], 1))
    held_user, held_item = asks[:, 0], asks[:, 1]
    found_item = item_factor.at[held_item].get(mode="promise_in_bounds")
    items = to_all(found_item)
    found_user = user_factor.at[held_user].get(mode="promise_in_bounds")
    step_cores = jnp.einsum("pqr,sr->spq", core, time_factor, precision=HIGH)
    found_user, items, step_cores = lax.optimization_barrier((found_user, items, step_cores))
    users = to_all(found_user)
    gram, moved, mixed, right = item_call(
        tile_users, tile_items, tile_steps, tile_count, items, step_cores, tile_values
    )
    slot_left = user_grad_call(users, gram, moved)
    users, slot_left = lax.optimization_barrier((users, slot_left))
    back_left = to_all(slot_left)
    slot_right, step_sums = tile_call(
        tile_users, tile_items, tile_steps, tile_count, users, right, step_cores, tile_values, mixed
    )
    part = rank * rank // owners
    parts = step_sums.reshape(step_count, owners, part).transpose(1, 0, 2)
    row = lax.dynamic_slice_in_dim(time_factor, lax.axis_index("rows"), 1, 0)
    row = jnp.broadcast_to(jnp.pad(row, ((0, 0), (0, width - rank)))[None], (owners, 1, width))
    blank = jnp.zeros((owners, 1, width), F32)
    sent = cat([parts.reshape(owners, -1, width), row, blank], 1)
    sent, back_left = lax.optimization_barrier((sent, back_left))
    got = to_all(sent)
    got, slot_right, step_sums = lax.optimization_barrier((got, slot_right, step_sums))
    back_right = to_all(slot_right)
    some = got[:, : step_count * part // width].reshape(count_tm, count_rows, step_count, part)
    some = jnp.sum(some, axis=1).reshape(count_tm * step_count, part)
    every_time = got[:, step_count * part // width, :rank]
    own = core_scale * jnp.einsum("sk,sr->kr", some, every_time, precision=HIGH)
    grad_core = lax.all_gather(own, AXES, axis=0, tiled=True).reshape(rank, rank, rank)
    own_time = jnp.einsum("spq,pqr->sr", step_sums, core, precision=HIGH)
    grad_time = time_scale * lax.psum(own_time, "rows")
    grad_users = owner_sum(held_user, back_left, blocks_own)
    grad_items = owner_sum(held_item, back_right, blocks_own)
    return (grad_users, grad_items, grad_time, grad_core)


def solution(mesh):
    in_specs = (
        P(AXES, None, None),
        P(AXES),
        P(AXES),
        P(AXES),
        P(AXES),
        P(AXES, None),
        P(AXES, None),
        P(AXES, None, None),
        P(AXES, None, None),
        P("tm", None),
        P(),
    )
    out_specs = (P(AXES, None, None), P(AXES, None, None), P("tm", None), P())
    return jax.shard_map(shards, mesh=mesh, in_specs=in_specs, out_specs=out_specs, check_vma=False)
```

```python
import functools

import jax
import jax.numpy as jnp
from jax import lax
from jax.experimental import pallas as pl
from jax.experimental.pallas import tpu as pltpu
from jax.sharding import PartitionSpec as P

HIGH = lax.Precision.HIGHEST
user_scale = 0.125
time_scale = 1.0 / 2048.0
core_scale = 1.0 / 4096.0

BF = jnp.bfloat16
F32 = jnp.float32
AXES = ("tm", "rows")
cat = jnp.concatenate
PREP = 8


def split(x):
    hi = x.astype(BF)
    lo = (x - hi.astype(F32)).astype(BF)
    return hi, lo


def mul(a, b):
    return lax.dot_general(a, b, (((1,), (0,)), ((), ())), preferred_element_type=F32)


def mul_t(a, b):
    return lax.dot_general(a, b, (((1,), (1,)), ((), ())), preferred_element_type=F32)


def twice(x):
    return cat([x, x], 1)


def quad(hi, lo):
    return cat([hi, hi, lo, lo], 0)


def pairs(hi, lo):
    return cat([twice(hi), twice(lo)], 0)


def whole(shape):
    return pl.BlockSpec(shape, lambda b, *_: (0,) * len(shape), pipeline_mode=pl.Buffered(1))


def live_block(group):
    def at(b, *scalars):
        last = jnp.maximum((scalars[-1][0] + group - 1) // group - 1, 0)
        return (jnp.minimum(b, last), 0, 0)
    return at


def params():
    return pltpu.CompilerParams(vmem_limit_bytes=60 * 2**20, dimension_semantics=("arbitrary",))


def in_groups(total, size, step):
    def one(g, carry):
        step([g * size + t for t in range(size)])
        return carry
    lax.fori_loop(0, total // size, one, 0)


def item_kernel(group, slots_user, slots_item, steps, count, items, cores, values,
                gram, moved, mixed_out, right, core_hl, gram_sum):
    rank, width = items.shape[1], items.shape[2]
    block = pl.program_id(0)

    @pl.when(block == 0)
    def _():
        def prep(ks):
            out = [cat(split(items[k]), 0) for k in ks]
            for k, x in zip(ks, out):
                right[k] = x
            for k in ks:
                gram_sum[k] = jnp.zeros_like(gram_sum[k])
                moved[k] = jnp.zeros_like(moved[k])
        in_groups(items.shape[0], PREP, prep)
        for k in range(cores.shape[0]):
            core_hl[k] = cat(split(cores[k]), 1)

    @pl.when(block * group < count[0])
    def _():
        span = range(group)
        tile = [block * group + t for t in span]
        user = [slots_user[k] for k in tile]
        mixed = []
        for t in span:
            r = right[slots_item[tile[t]]]
            mixed.append(mul(twice(core_hl[steps[tile[t]]]), quad(r[:rank], r[rank:])))
        mixed = [split(jnp.where(tile[t] < count[0], mixed[t], 0.0)) for t in span]
        both = []
        for t in span:
            v = values[t]
            both.append(mul_t(cat(mixed[t], 1), cat([twice(v), pairs(*mixed[t])], 0)))
        for t in span:
            mixed_out[t] = cat(mixed[t], 0)
        for t in span:
            moved[user[t]] += both[t][:, :width]
            gram_sum[user[t]] += both[t][:, width:]

    @pl.when(block == pl.num_programs(0) - 1)
    def _():
        def finish(ks):
            out = [gram_sum[k] for k in ks]
            out = [cat(split(x[:, :rank] + x[:, rank:]), 1) for x in out]
            for k, x in zip(ks, out):
                gram[k] = x
        in_groups(gram.shape[0], PREP, finish)


def item_call(slots_user, slots_item, steps, count, items, cores, values, group=32):
    slots, width = values.shape[:2]
    held, rank = items.shape[:2]
    return pl.pallas_call(
        functools.partial(item_kernel, group),
        grid_spec=pltpu.PrefetchScalarGridSpec(
            num_scalar_prefetch=4,
            grid=(slots // group,),
            in_specs=[whole(items.shape), whole(cores.shape),
                      pl.BlockSpec((group, width, width), live_block(group))],
            out_specs=[whole((held, rank, 2 * rank)), whole((held, rank, width)),
                       pl.BlockSpec((group, 2 * rank, width), live_block(group)),
                       whole((held, 2 * rank, width))],
            scratch_shapes=[pltpu.VMEM((cores.shape[0], rank, 2 * rank), BF),
                            pltpu.VMEM((held, rank, 2 * rank), F32)],
        ),
        out_shape=[jax.ShapeDtypeStruct((held, rank, 2 * rank), BF),
                   jax.ShapeDtypeStruct((held, rank, width), F32),
                   jax.ShapeDtypeStruct((slots, 2 * rank, width), BF),
                   jax.ShapeDtypeStruct((held, 2 * rank, width), BF)],
        compiler_params=params(),
        cost_estimate=pl.CostEstimate(flops=2 * 10**10, bytes_accessed=5 * 10**7, transcendentals=0),
        name="item_side",
    )(slots_user, slots_item, steps, count, items, cores, values)


def user_grad_kernel(group, users, gram, moved, grad):
    span = range(group)
    out = [mul(twice(gram[t]), quad(*split(users[t]))) for t in span]
    for t in span:
        grad[t] = out[t] - moved[t]


def user_grad_call(users, gram, moved, group=64):
    held, rank, width = users.shape
    block = pl.BlockSpec((group, rank, width), lambda b: (b, 0, 0))
    return pl.pallas_call(
        functools.partial(user_grad_kernel, group),
        grid=(held // group,),
        in_specs=[block, pl.BlockSpec((group, rank, 2 * rank), lambda b: (b, 0, 0)), block],
        out_specs=block,
        out_shape=jax.ShapeDtypeStruct(users.shape, F32),
        compiler_params=params(),
        cost_estimate=pl.CostEstimate(flops=10**9, bytes_accessed=2 * 10**7, transcendentals=0),
        name="user_grad",
    )(users, gram, moved)


def tile_kernel(group, slots_user, slots_item, steps, count, users, right, cores, values, mixed,
                grad, sums, left, core_t, sums_hl):
    rank, width = users.shape[1], users.shape[2]
    block = pl.program_id(0)

    @pl.when(block == 0)
    def _():
        def prep(ks):
            x = [split(users[k]) for k in ks]
            h = [mul_t(cat(y, 1), pairs(*y)) for y in x]
            h = [cat(split(y[:, :rank] + y[:, rank:]), 1) for y in h]
            for k, y, z in zip(ks, x, h):
                left[k] = cat([-y[0], -y[1], z], 1)
                grad[k, :rank] = jnp.zeros((rank, width), F32)
        in_groups(users.shape[0], PREP, prep)
        for k in range(cores.shape[0]):
            core_t[k] = cat(split(cores[k].T), 1)
        sums_hl[...] = jnp.zeros_like(sums_hl)

    @pl.when(block * group < count[0])
    def _():
        span = range(group)
        tile = [block * group + t for t in span]
        item = [slots_item[k] for k in tile]
        step = [steps[k] for k in tile]
        inner = []
        for t in span:
            x = left[slots_user[tile[t]]]
            v, m = values[t], mixed[t]
            inner.append(mul(cat([x, x[:, 2 * width:]], 1), cat([v, v, quad(m[:rank], m[rank:])], 0)))
        inner = [split(jnp.where(tile[t] < count[0], inner[t], 0.0)) for t in span]
        grad_v = [mul(twice(core_t[step[t]]), quad(*inner[t])) for t in span]
        dcore = []
        for t in span:
            a = mul_t(cat(inner[t], 0), right[item[t]])
            dcore.append(a[:rank] + a[rank:])
        for t in span:
            grad[item[t], :rank] += grad_v[t]
            sums_hl[step[t]] += dcore[t]

    @pl.when(block == pl.num_programs(0) - 1)
    def _():
        for k in range(sums.shape[0]):
            a = sums_hl[k]
            sums[k] = a[:, :rank] + a[:, rank:]


def tile_call(slots_user, slots_item, steps, count, users, right, cores, values, mixed, extra, group=32):
    slots, width = values.shape[:2]
    held, rank = users.shape[:2]
    return pl.pallas_call(
        functools.partial(tile_kernel, group),
        grid_spec=pltpu.PrefetchScalarGridSpec(
            num_scalar_prefetch=4,
            grid=(slots // group,),
            in_specs=[whole(users.shape), whole(right.shape), whole(cores.shape),
                      pl.BlockSpec((group, width, width), live_block(group)),
                      pl.BlockSpec((group, 2 * rank, width), live_block(group))],
            out_specs=[whole((held, rank + extra, width)), whole(cores.shape)],
            scratch_shapes=[pltpu.VMEM((held, rank, 2 * width + 2 * rank), BF),
                            pltpu.VMEM((cores.shape[0], rank, 2 * rank), BF),
                            pltpu.VMEM((cores.shape[0], rank, 2 * rank), F32)],
        ),
        out_shape=[jax.ShapeDtypeStruct((held, rank + extra, width), F32),
                   jax.ShapeDtypeStruct(cores.shape, F32)],
        compiler_params=params(),
        cost_estimate=pl.CostEstimate(flops=3 * 10**10, bytes_accessed=5 * 10**7, transcendentals=0),
        name="tile_side",
    )(slots_user, slots_item, steps, count, users, right, cores, values, mixed)

def ask_kernel(group, held, table, out):
    block = pl.program_id(0)
    for t in range(group):
        out[t] = table[held[block * group + t]]


def asked(held, table, group=16):
    total = held.shape[0]
    return pl.pallas_call(
        functools.partial(ask_kernel, group),
        grid_spec=pltpu.PrefetchScalarGridSpec(
            num_scalar_prefetch=1,
            grid=(total // group,),
            in_specs=[whole(table.shape)],
            out_specs=pl.BlockSpec((group,) + table.shape[1:], lambda b, *_: (b, 0, 0)),
        ),
        out_shape=jax.ShapeDtypeStruct((total,) + table.shape[1:], F32),
        compiler_params=params(),
        cost_estimate=pl.CostEstimate(flops=0, bytes_accessed=10**7, transcendentals=0),
        name="asked",
    )(held, table)


ADDERS = 4


def owner_kernel(group, rank, scale, held, back, out, *rest):
    block = pl.program_id(0)
    core, adders = (rest[0], rest[1:]) if len(rest) > ADDERS else (None, rest)

    @pl.when(block == 0)
    def _():
        for a in adders:
            a[...] = jnp.zeros_like(a)

    for t in range(0, group, ADDERS):
        at = [held[block * group + t + k] for k in range(ADDERS)]
        new = [adders[k][at[k]] + back[t + k, :rank] for k in range(ADDERS)]
        for k in range(ADDERS):
            adders[k][at[k]] = new[k]
    if core is not None:
        half = back.shape[2] // 2
        new = [back[t, rank:] for t in range(group)]
        new = [cat([x[:, :half], x[:, half:]], 0) for x in new]
        size = new[0].shape[0]
        for t in range(group):
            core[t * size : (t + 1) * size] = new[t]

    @pl.when(block == pl.num_programs(0) - 1)
    def _():
        total = adders[0][...]
        for a in adders[1:]:
            total = total + a[...]
        out[...] = scale * total


def owner_sum(held, back, blocks_own, rank, scale, group=16):
    total, rows, width = back.shape
    out_specs = [pl.BlockSpec((blocks_own, rank, width), lambda b, *_: (0, 0, 0))]
    out_shape = [jax.ShapeDtypeStruct((blocks_own, rank, width), F32)]
    if rows > rank:
        part = 2 * (rows - rank)
        out_specs.append(pl.BlockSpec((group * part, width // 2), lambda b, *_: (b, 0)))
        out_shape.append(jax.ShapeDtypeStruct((total * part, width // 2), F32))
    return pl.pallas_call(
        functools.partial(owner_kernel, group, rank, scale),
        grid_spec=pltpu.PrefetchScalarGridSpec(
            num_scalar_prefetch=1,
            grid=(total // group,),
            in_specs=[pl.BlockSpec((group, rows, width), lambda b, *_: (b, 0, 0))],
            out_specs=out_specs,
            scratch_shapes=[pltpu.VMEM((blocks_own, rank, width), F32) for _ in range(ADDERS)],
        ),
        out_shape=out_shape,
        compiler_params=params(),
        cost_estimate=pl.CostEstimate(flops=10**7, bytes_accessed=10**7, transcendentals=0),
        name="owner_sum",
    )(held, back)


def to_all(x):
    return lax.all_to_all(x, AXES, split_axis=0, concat_axis=0, tiled=True)


def shards(
    tile_values,
    tile_users,
    tile_items,
    tile_steps,
    tile_count,
    users_ask,
    items_ask,
    user_factor,
    item_factor,
    time_factor,
    core,
):
    rank = user_factor.shape[1]
    width = user_factor.shape[2]
    blocks_own = user_factor.shape[0]
    step_count = time_factor.shape[0]
    count_tm = lax.axis_size("tm")
    count_rows = lax.axis_size("rows")
    owners = count_tm * count_rows
    part = rank * rank // owners
    sum_rows = step_count * part // width
    time_rows = step_count * rank // width
    core_rows = part * rank // width
    asks = to_all(cat([users_ask, items_ask], 1))
    held_user, held_item = asks[:, 0], asks[:, 1]
    items = to_all(asked(held_item, item_factor))
    found_user = asked(held_user, user_factor)
    step_cores = jnp.einsum("pqr,sr->spq", core, time_factor, precision=HIGH)
    found_user, items, step_cores = lax.optimization_barrier((found_user, items, step_cores))
    users = to_all(found_user)
    gram, moved, mixed, right = item_call(
        tile_users, tile_items, tile_steps, tile_count, items, step_cores, tile_values
    )
    slot_left = user_grad_call(users, gram, moved)
    users, slot_left = lax.optimization_barrier((users, slot_left))
    back_left = to_all(slot_left)
    slot_right, step_sums = tile_call(
        tile_users, tile_items, tile_steps, tile_count, users, right, step_cores, tile_values, mixed, core_rows
    )
    parts = step_sums.reshape(step_count, owners, part).transpose(1, 0, 2).reshape(owners, sum_rows, width)
    row = lax.dynamic_slice_in_dim(time_factor, lax.axis_index("rows"), 1, 0)
    row = jnp.pad(row, ((0, 0), (0, width - rank)))
    own_time = jnp.einsum("spq,pqr->sr", step_sums, core, precision=HIGH).reshape(time_rows, width)
    blank = jnp.zeros((-(sum_rows + 1 + time_rows) % 8, width), F32)
    shared = cat([row, own_time, blank], 0)
    sent = cat([parts, jnp.broadcast_to(shared[None], (owners,) + shared.shape)], 1)
    sent, back_left = lax.optimization_barrier((sent, back_left))
    got = to_all(sent)
    some = got[:, :sum_rows].reshape(count_tm, count_rows, step_count, part)
    some = jnp.sum(some, axis=1).reshape(count_tm * step_count, part)
    every_time = got[:, sum_rows, :rank]
    own = core_scale * jnp.einsum("sk,sr->kr", some, every_time, precision=HIGH)
    own = cat([own[:core_rows], own[core_rows:]], 1)
    slot_right = slot_right.at[:, rank:].set(jnp.broadcast_to(own[None], (owners, core_rows, width)))
    back_right = to_all(slot_right)
    first = lax.axis_index("tm") * count_rows
    terms = lax.dynamic_slice_in_dim(got, first, count_rows, 0)[:, sum_rows + 1 : sum_rows + 1 + time_rows]
    grad_time = time_scale * jnp.sum(terms, axis=0).reshape(step_count, rank)
    (grad_users,) = owner_sum(held_user, back_left, blocks_own, rank, user_scale)
    grad_items, grad_core = owner_sum(held_item, back_right, blocks_own, rank, user_scale)
    grad_core = grad_core.reshape(rank, rank, rank)
    return (grad_users, grad_items, grad_time, grad_core)


def solution(mesh):
    in_specs = (
        P(AXES, None, None),
        P(AXES),
        P(AXES),
        P(AXES),
        P(AXES),
        P(AXES, None),
        P(AXES, None),
        P(AXES, None, None),
        P(AXES, None, None),
        P("tm", None),
        P(),
    )
    out_specs = (P(AXES, None, None), P(AXES, None, None), P("tm", None), P())
    return jax.shard_map(shards, mesh=mesh, in_specs=in_specs, out_specs=out_specs, check_vma=False)
```

```python
import functools

import jax
import jax.numpy as jnp
from jax import lax
from jax.experimental import pallas as pl
from jax.experimental.pallas import tpu as pltpu
from jax.sharding import PartitionSpec as P

HIGH = lax.Precision.HIGHEST
user_scale = 0.125
time_scale = 1.0 / 2048.0
core_scale = 1.0 / 4096.0

BF = jnp.bfloat16
F32 = jnp.float32
AXES = ("tm", "rows")
cat = jnp.concatenate
PREP = 8


def split(x):
    hi = x.astype(BF)
    lo = (x - hi.astype(F32)).astype(BF)
    return hi, lo


def mul(a, b):
    return lax.dot_general(a, b, (((1,), (0,)), ((), ())), preferred_element_type=F32)


def mul_t(a, b):
    return lax.dot_general(a, b, (((1,), (1,)), ((), ())), preferred_element_type=F32)


def twice(x):
    return cat([x, x], 1)


def quad(hi, lo):
    return cat([hi, hi, lo, lo], 0)


def pairs(hi, lo):
    return cat([twice(hi), twice(lo)], 0)


def whole(shape):
    return pl.BlockSpec(shape, lambda b, *_: (0,) * len(shape), pipeline_mode=pl.Buffered(1))


def live_block(group):
    def at(b, *scalars):
        last = jnp.maximum((scalars[-1][0] + group - 1) // group - 1, 0)
        return (jnp.minimum(b, last), 0, 0)
    return at


def params():
    return pltpu.CompilerParams(vmem_limit_bytes=60 * 2**20, dimension_semantics=("arbitrary",))


def in_groups(total, size, step):
    def one(g, carry):
        step([g * size + t for t in range(size)])
        return carry
    lax.fori_loop(0, total // size, one, 0)


def item_kernel(group, slots_user, slots_item, steps, count, items, cores, values,
                gram, moved, mixed_out, right, core_hl, gram_sum):
    rank, width = items.shape[1], items.shape[2]
    block = pl.program_id(0)

    @pl.when(block == 0)
    def _():
        def prep(ks):
            out = [cat(split(items[k]), 0) for k in ks]
            for k, x in zip(ks, out):
                right[k] = x
            for k in ks:
                gram_sum[k] = jnp.zeros_like(gram_sum[k])
                moved[k] = jnp.zeros_like(moved[k])
        in_groups(items.shape[0], PREP, prep)
        for k in range(cores.shape[0]):
            core_hl[k] = cat(split(cores[k]), 1)

    @pl.when(block * group < count[0])
    def _():
        span = range(group)
        tile = [block * group + t for t in span]
        user = [slots_user[k] for k in tile]
        mixed = []
        for t in span:
            r = right[slots_item[tile[t]]]
            mixed.append(mul(twice(core_hl[steps[tile[t]]]), quad(r[:rank], r[rank:])))
        mixed = [split(jnp.where(tile[t] < count[0], mixed[t], 0.0)) for t in span]
        both = []
        for t in span:
            v = values[t]
            both.append(mul_t(cat(mixed[t], 1), cat([twice(v), pairs(*mixed[t])], 0)))
        for t in span:
            mixed_out[t] = cat(mixed[t], 0)
        for t in span:
            moved[user[t]] += both[t][:, :width]
            gram_sum[user[t]] += both[t][:, width:]

    @pl.when(block == pl.num_programs(0) - 1)
    def _():
        def finish(ks):
            out = [gram_sum[k] for k in ks]
            out = [cat(split(x[:, :rank] + x[:, rank:]), 1) for x in out]
            for k, x in zip(ks, out):
                gram[k] = x
        in_groups(gram.shape[0], PREP, finish)


def item_call(slots_user, slots_item, steps, count, items, cores, values, group=32):
    slots, width = values.shape[:2]
    held, rank = items.shape[:2]
    return pl.pallas_call(
        functools.partial(item_kernel, group),
        grid_spec=pltpu.PrefetchScalarGridSpec(
            num_scalar_prefetch=4,
            grid=(slots // group,),
            in_specs=[whole(items.shape), whole(cores.shape),
                      pl.BlockSpec((group, width, width), live_block(group))],
            out_specs=[whole((held, rank, 2 * rank)), whole((held, rank, width)),
                       pl.BlockSpec((group, 2 * rank, width), live_block(group)),
                       whole((held, 2 * rank, width))],
            scratch_shapes=[pltpu.VMEM((cores.shape[0], rank, 2 * rank), BF),
                            pltpu.VMEM((held, rank, 2 * rank), F32)],
        ),
        out_shape=[jax.ShapeDtypeStruct((held, rank, 2 * rank), BF),
                   jax.ShapeDtypeStruct((held, rank, width), F32),
                   jax.ShapeDtypeStruct((slots, 2 * rank, width), BF),
                   jax.ShapeDtypeStruct((held, 2 * rank, width), BF)],
        compiler_params=params(),
        cost_estimate=pl.CostEstimate(flops=2 * 10**10, bytes_accessed=5 * 10**7, transcendentals=0),
        name="item_side",
    )(slots_user, slots_item, steps, count, items, cores, values)


CHUNKS = 8


def user_grad_kernel(users, gram, moved, grad, users_v, gram_v, moved_v, grad_v, sems):
    size = users_v.shape[0] // CHUNKS

    def copies(c):
        at = pl.ds(c * size, size)
        pieces = ((users, users_v), (gram, gram_v), (moved, moved_v))
        return [pltpu.make_async_copy(a.at[at], b.at[at], sems.at[k, c]) for k, (a, b) in enumerate(pieces)]

    def back(c):
        at = pl.ds(c * size, size)
        return pltpu.make_async_copy(grad_v.at[at], grad.at[at], sems.at[3, c])

    for c in range(CHUNKS):
        for copy in copies(c):
            copy.start()
    for c in range(CHUNKS):
        for copy in copies(c):
            copy.wait()
        span = range(c * size, (c + 1) * size)
        out = [mul(twice(gram_v[t]), quad(*split(users_v[t]))) for t in span]
        for t, x in zip(span, out):
            grad_v[t] = x - moved_v[t]
        back(c).start()
    for c in range(CHUNKS):
        back(c).wait()


def user_grad_call(users, gram, moved):
    any_space = pl.BlockSpec(memory_space=pl.ANY)
    return pl.pallas_call(
        user_grad_kernel,
        in_specs=[any_space] * 3,
        out_specs=any_space,
        out_shape=jax.ShapeDtypeStruct(users.shape, F32),
        scratch_shapes=[
            pltpu.VMEM(users.shape, F32),
            pltpu.VMEM(gram.shape, BF),
            pltpu.VMEM(users.shape, F32),
            pltpu.VMEM(users.shape, F32),
            pltpu.SemaphoreType.DMA((4, CHUNKS)),
        ],
        compiler_params=pltpu.CompilerParams(vmem_limit_bytes=60 * 2**20),
        cost_estimate=pl.CostEstimate(flops=10**9, bytes_accessed=2 * 10**7, transcendentals=0),
        name="user_grad",
    )(users, gram, moved)


def tile_kernel(group, slots_user, slots_item, steps, count, users, right, cores, values, mixed,
                grad, sums, left, core_t, sums_hl):
    rank, width = users.shape[1], users.shape[2]
    block = pl.program_id(0)

    @pl.when(block == 0)
    def _():
        def prep(ks):
            x = [split(users[k]) for k in ks]
            h = [mul_t(cat(y, 1), pairs(*y)) for y in x]
            h = [cat(split(y[:, :rank] + y[:, rank:]), 1) for y in h]
            for k, y, z in zip(ks, x, h):
                left[k] = cat([-y[0], -y[1], z], 1)
                grad[k, :rank] = jnp.zeros((rank, width), F32)
        in_groups(users.shape[0], PREP, prep)
        for k in range(cores.shape[0]):
            core_t[k] = cat(split(cores[k].T), 1)
        sums_hl[...] = jnp.zeros_like(sums_hl)

    @pl.when(block * group < count[0])
    def _():
        span = range(group)
        tile = [block * group + t for t in span]
        item = [slots_item[k] for k in tile]
        step = [steps[k] for k in tile]
        inner = []
        for t in span:
            x = left[slots_user[tile[t]]]
            v, m = values[t], mixed[t]
            inner.append(mul(cat([x, x[:, 2 * width:]], 1), cat([v, v, quad(m[:rank], m[rank:])], 0)))
        inner = [split(jnp.where(tile[t] < count[0], inner[t], 0.0)) for t in span]
        grad_v = [mul(twice(core_t[step[t]]), quad(*inner[t])) for t in span]
        dcore = []
        for t in span:
            a = mul_t(cat(inner[t], 0), right[item[t]])
            dcore.append(a[:rank] + a[rank:])
        for t in span:
            grad[item[t], :rank] += grad_v[t]
            sums_hl[step[t]] += dcore[t]

    @pl.when(block == pl.num_programs(0) - 1)
    def _():
        for k in range(sums.shape[0]):
            a = sums_hl[k]
            sums[k] = a[:, :rank] + a[:, rank:]


def tile_call(slots_user, slots_item, steps, count, users, right, cores, values, mixed, extra, group=32):
    slots, width = values.shape[:2]
    held, rank = users.shape[:2]
    return pl.pallas_call(
        functools.partial(tile_kernel, group),
        grid_spec=pltpu.PrefetchScalarGridSpec(
            num_scalar_prefetch=4,
            grid=(slots // group,),
            in_specs=[whole(users.shape), whole(right.shape), whole(cores.shape),
                      pl.BlockSpec((group, width, width), live_block(group)),
                      pl.BlockSpec((group, 2 * rank, width), live_block(group))],
            out_specs=[whole((held, rank + extra, width)), whole(cores.shape)],
            scratch_shapes=[pltpu.VMEM((held, rank, 2 * width + 2 * rank), BF),
                            pltpu.VMEM((cores.shape[0], rank, 2 * rank), BF),
                            pltpu.VMEM((cores.shape[0], rank, 2 * rank), F32)],
        ),
        out_shape=[jax.ShapeDtypeStruct((held, rank + extra, width), F32),
                   jax.ShapeDtypeStruct(cores.shape, F32)],
        compiler_params=params(),
        cost_estimate=pl.CostEstimate(flops=3 * 10**10, bytes_accessed=5 * 10**7, transcendentals=0),
        name="tile_side",
    )(slots_user, slots_item, steps, count, users, right, cores, values, mixed)

def ask_kernel(held, table, out, buffer, sems):
    size = buffer.shape[0] // CHUNKS

    def send(c):
        at = pl.ds(c * size, size)
        return pltpu.make_async_copy(buffer.at[at], out.at[at], sems.at[c])

    for c in range(CHUNKS):
        for t in range(c * size, (c + 1) * size, 4):
            new = [table[held[t + k]] for k in range(4)]
            for k in range(4):
                buffer[t + k] = new[k]
        send(c).start()
    for c in range(CHUNKS):
        send(c).wait()


def asked(held, table):
    shape = (held.shape[0],) + table.shape[1:]
    return pl.pallas_call(
        ask_kernel,
        in_specs=[pl.BlockSpec(memory_space=pltpu.SMEM), pl.BlockSpec(memory_space=pltpu.VMEM)],
        out_specs=pl.BlockSpec(memory_space=pl.ANY),
        out_shape=jax.ShapeDtypeStruct(shape, F32),
        scratch_shapes=[pltpu.VMEM(shape, F32), pltpu.SemaphoreType.DMA((CHUNKS,))],
        compiler_params=pltpu.CompilerParams(vmem_limit_bytes=60 * 2**20),
        cost_estimate=pl.CostEstimate(flops=0, bytes_accessed=10**7, transcendentals=0),
        name="asked",
    )(held, table)


ADDERS = 4


def owner_kernel(rank, scale, held, back, out, *rest):
    adders, (back_v, sems) = rest[:ADDERS], rest[ADDERS:]
    size = back_v.shape[0] // CHUNKS

    def fetch(c):
        at = pl.ds(c * size, size)
        return pltpu.make_async_copy(back.at[at, pl.ds(0, rank)], back_v.at[at], sems.at[c])

    for c in range(CHUNKS):
        fetch(c).start()
    for a in adders:
        a[...] = jnp.zeros_like(a)
    for c in range(CHUNKS):
        fetch(c).wait()
        for t in range(c * size, (c + 1) * size, ADDERS):
            at = [held[t + k] for k in range(ADDERS)]
            new = [adders[k][at[k]] + back_v[t + k] for k in range(ADDERS)]
            for k in range(ADDERS):
                adders[k][at[k]] = new[k]
    total = adders[0][...]
    for a in adders[1:]:
        total = total + a[...]
    out[...] = scale * total


def owner_sum(held, back, blocks_own, rank, scale):
    total, rows, width = back.shape
    return pl.pallas_call(
        functools.partial(owner_kernel, rank, scale),
        in_specs=[pl.BlockSpec(memory_space=pltpu.SMEM), pl.BlockSpec(memory_space=pl.ANY)],
        out_specs=pl.BlockSpec(memory_space=pltpu.VMEM),
        out_shape=jax.ShapeDtypeStruct((blocks_own, rank, width), F32),
        scratch_shapes=[pltpu.VMEM((blocks_own, rank, width), F32) for _ in range(ADDERS)]
        + [pltpu.VMEM((total, rank, width), F32), pltpu.SemaphoreType.DMA((CHUNKS,))],
        compiler_params=pltpu.CompilerParams(vmem_limit_bytes=60 * 2**20),
        cost_estimate=pl.CostEstimate(flops=10**7, bytes_accessed=10**7, transcendentals=0),
        name="owner_sum",
    )(held, back)


def core_kernel(odd, mine, other, core):
    half = mine.shape[2] // 2
    rows = 2 * mine.shape[1]

    def step(ks):
        a = [mine[k] for k in ks]
        b = [other[k] for k in ks]
        new = []
        for x, y in zip(a, b):
            new.append((jnp.where(odd[0] == 0, x, y), jnp.where(odd[0] == 0, y, x)))
        new = [[cat([x[:, :half], x[:, half:]], 0) for x in pair] for pair in new]
        for k, (x, y) in zip(ks, new):
            core[k, :rows] = x
            core[k, rows:] = y

    for g in range(0, mine.shape[0], PREP):
        step(range(g, g + PREP))


def core_unpack(odd, mine, other):
    owners, rows, width = mine.shape
    return pl.pallas_call(
        core_kernel,
        in_specs=[pl.BlockSpec(memory_space=pltpu.SMEM)] + [pl.BlockSpec(memory_space=pltpu.VMEM)] * 2,
        out_specs=pl.BlockSpec(memory_space=pltpu.VMEM),
        out_shape=jax.ShapeDtypeStruct((owners, 4 * rows, width // 2), F32),
        compiler_params=pltpu.CompilerParams(vmem_limit_bytes=60 * 2**20),
        cost_estimate=pl.CostEstimate(flops=10**6, bytes_accessed=3 * 10**6, transcendentals=0),
        name="core_unpack",
    )(odd, mine, other)


def to_all(x):
    return lax.all_to_all(x, AXES, split_axis=0, concat_axis=0, tiled=True)


def shards(
    tile_values,
    tile_users,
    tile_items,
    tile_steps,
    tile_count,
    users_ask,
    items_ask,
    user_factor,
    item_factor,
    time_factor,
    core,
):
    rank = user_factor.shape[1]
    width = user_factor.shape[2]
    blocks_own = user_factor.shape[0]
    step_count = time_factor.shape[0]
    count_tm = lax.axis_size("tm")
    count_rows = lax.axis_size("rows")
    owners = count_tm * count_rows
    part = rank * rank // owners
    sum_rows = step_count * part // width
    time_rows = step_count * rank // width
    core_rows = part * rank // width // 2
    asks = to_all(cat([users_ask, items_ask], 1))
    held_user, held_item = asks[:, 0], asks[:, 1]
    items = to_all(asked(held_item, item_factor))
    found_user = asked(held_user, user_factor)
    step_cores = jnp.einsum("pqr,sr->spq", core, time_factor, precision=HIGH)
    found_user, items, step_cores = lax.optimization_barrier((found_user, items, step_cores))
    users = to_all(found_user)
    gram, moved, mixed, right = item_call(
        tile_users, tile_items, tile_steps, tile_count, items, step_cores, tile_values
    )
    slot_left = user_grad_call(users, gram, moved)
    users, slot_left = lax.optimization_barrier((users, slot_left))
    back_left = to_all(slot_left)
    slot_right, step_sums = tile_call(
        tile_users, tile_items, tile_steps, tile_count, users, right, step_cores, tile_values, mixed, core_rows
    )
    parts = step_sums.reshape(step_count, owners, part).transpose(1, 0, 2).reshape(owners, sum_rows, width)
    row = lax.dynamic_slice_in_dim(time_factor, lax.axis_index("rows"), 1, 0)
    row = jnp.pad(row, ((0, 0), (0, width - rank)))
    own_time = jnp.einsum("spq,pqr->sr", step_sums, core, precision=HIGH).reshape(time_rows, width)
    blank = jnp.zeros((-(sum_rows + 1 + time_rows) % 8, width), F32)
    shared = cat([row, own_time, blank], 0)
    sent = cat([parts, jnp.broadcast_to(shared[None], (owners,) + shared.shape)], 1)
    sent, back_left = lax.optimization_barrier((sent, back_left))
    got = to_all(sent)
    some = got[:, :sum_rows].reshape(count_tm, count_rows, step_count, part)
    some = jnp.sum(some, axis=1).reshape(count_tm * step_count, part)
    every_time = got[:, sum_rows, :rank]
    own = core_scale * jnp.einsum("sk,sr->kr", some, every_time, precision=HIGH)
    own = own.reshape(2, 2, core_rows, rank).transpose(0, 2, 1, 3).reshape(1, 2, core_rows, width)
    own = jnp.broadcast_to(own, (owners // 2, 2, core_rows, width)).reshape(owners, core_rows, width)
    slot_right = slot_right.at[:, rank:].set(own)
    back_right = to_all(slot_right)
    first = lax.axis_index("tm") * count_rows
    terms = lax.dynamic_slice_in_dim(got, first, count_rows, 0)[:, sum_rows + 1 : sum_rows + 1 + time_rows]
    grad_time = time_scale * jnp.sum(terms, axis=0).reshape(step_count, rank)
    grad_users = owner_sum(held_user, back_left, blocks_own, rank, user_scale)
    back_right, grad_users, grad_time = lax.optimization_barrier((back_right, grad_users, grad_time))
    mine = back_right[:, rank:]
    other = lax.ppermute(mine, "rows", [(r, r ^ 1) for r in range(count_rows)])
    grad_items = owner_sum(held_item, back_right, blocks_own, rank, user_scale)
    odd = (lax.axis_index("rows") % 2).astype(jnp.int32).reshape(1)
    grad_core = core_unpack(odd, mine, other).reshape(rank, rank, rank)
    return (grad_users, grad_items, grad_time, grad_core)


def solution(mesh):
    in_specs = (
        P(AXES, None, None),
        P(AXES),
        P(AXES),
        P(AXES),
        P(AXES),
        P(AXES, None),
        P(AXES, None),
        P(AXES, None, None),
        P(AXES, None, None),
        P("tm", None),
        P(),
    )
    out_specs = (P(AXES, None, None), P(AXES, None, None), P("tm", None), P())
    return jax.shard_map(shards, mesh=mesh, in_specs=in_specs, out_specs=out_specs, check_vma=False)
```

```python
import functools

import jax
import jax.numpy as jnp
from jax import lax
from jax.experimental import pallas as pl
from jax.experimental.pallas import tpu as pltpu
from jax.sharding import PartitionSpec as P

HIGH = lax.Precision.HIGHEST
user_scale = 0.125
time_scale = 1.0 / 2048.0
core_scale = 1.0 / 4096.0

BF = jnp.bfloat16
F32 = jnp.float32
AXES = ("tm", "rows")
cat = jnp.concatenate
PREP = 8


def split(x):
    hi = x.astype(BF)
    lo = (x - hi.astype(F32)).astype(BF)
    return hi, lo


def mul(a, b):
    return lax.dot_general(a, b, (((1,), (0,)), ((), ())), preferred_element_type=F32)


def mul_t(a, b):
    return lax.dot_general(a, b, (((1,), (1,)), ((), ())), preferred_element_type=F32)


def twice(x):
    return cat([x, x], 1)


def quad(hi, lo):
    return cat([hi, hi, lo, lo], 0)


def pairs(hi, lo):
    return cat([twice(hi), twice(lo)], 0)


def whole(shape):
    return pl.BlockSpec(shape, lambda b, *_: (0,) * len(shape), pipeline_mode=pl.Buffered(1))


def live_block(group):
    def at(b, *scalars):
        last = jnp.maximum((scalars[-1][0] + group - 1) // group - 1, 0)
        return (jnp.minimum(b, last), 0, 0)
    return at


def params():
    return pltpu.CompilerParams(vmem_limit_bytes=60 * 2**20, dimension_semantics=("arbitrary",))


def in_groups(total, size, step):
    def one(g, carry):
        step([g * size + t for t in range(size)])
        return carry
    lax.fori_loop(0, total // size, one, 0)


def item_kernel(group, slots_user, slots_item, steps, count, items, cores, values,
                gram, moved, mixed_out, right, core_hl, gram_sum):
    rank, width = items.shape[1], items.shape[2]
    block = pl.program_id(0)

    @pl.when(block == 0)
    def _():
        def prep(ks):
            out = [cat(split(items[k]), 0) for k in ks]
            for k, x in zip(ks, out):
                right[k] = x
            for k in ks:
                gram_sum[k] = jnp.zeros_like(gram_sum[k])
                moved[k] = jnp.zeros_like(moved[k])
        in_groups(items.shape[0], PREP, prep)
        for k in range(cores.shape[0]):
            core_hl[k] = cat(split(cores[k]), 1)

    @pl.when(block * group < count[0])
    def _():
        span = range(group)
        tile = [block * group + t for t in span]
        user = [slots_user[k] for k in tile]
        mixed = []
        for t in span:
            r = right[slots_item[tile[t]]]
            mixed.append(mul(twice(core_hl[steps[tile[t]]]), quad(r[:rank], r[rank:])))
        mixed = [split(jnp.where(tile[t] < count[0], mixed[t], 0.0)) for t in span]
        both = []
        for t in span:
            v = values[t]
            both.append(mul_t(cat(mixed[t], 1), cat([twice(v), pairs(*mixed[t])], 0)))
        for t in span:
            mixed_out[t] = cat(mixed[t], 0)
        for t in span:
            moved[user[t]] += both[t][:, :width]
            gram_sum[user[t]] += both[t][:, width:]

    @pl.when(block == pl.num_programs(0) - 1)
    def _():
        def finish(ks):
            out = [gram_sum[k] for k in ks]
            out = [cat(split(x[:, :rank] + x[:, rank:]), 1) for x in out]
            for k, x in zip(ks, out):
                gram[k] = x
        in_groups(gram.shape[0], PREP, finish)


def item_call(slots_user, slots_item, steps, count, items, cores, values, group=32):
    slots, width = values.shape[:2]
    held, rank = items.shape[:2]
    return pl.pallas_call(
        functools.partial(item_kernel, group),
        grid_spec=pltpu.PrefetchScalarGridSpec(
            num_scalar_prefetch=4,
            grid=(slots // group,),
            in_specs=[whole(items.shape), whole(cores.shape),
                      pl.BlockSpec((group, width, width), live_block(group))],
            out_specs=[whole((held, rank, 2 * rank)), whole((held, rank, width)),
                       pl.BlockSpec((group, 2 * rank, width), live_block(group)),
                       whole((held, 2 * rank, width))],
            scratch_shapes=[pltpu.VMEM((cores.shape[0], rank, 2 * rank), BF),
                            pltpu.VMEM((held, rank, 2 * rank), F32)],
        ),
        out_shape=[jax.ShapeDtypeStruct((held, rank, 2 * rank), BF),
                   jax.ShapeDtypeStruct((held, rank, width), F32),
                   jax.ShapeDtypeStruct((slots, 2 * rank, width), BF),
                   jax.ShapeDtypeStruct((held, 2 * rank, width), BF)],
        compiler_params=params(),
        cost_estimate=pl.CostEstimate(flops=2 * 10**10, bytes_accessed=5 * 10**7, transcendentals=0),
        name="item_side",
    )(slots_user, slots_item, steps, count, items, cores, values)


CHUNKS = 8


def user_grad_kernel(users, gram, moved, grad, users_v, gram_v, moved_v, grad_v, sems):
    size = users_v.shape[0] // CHUNKS

    def copies(c):
        at = pl.ds(c * size, size)
        pieces = ((users, users_v), (gram, gram_v), (moved, moved_v))
        return [pltpu.make_async_copy(a.at[at], b.at[at], sems.at[k, c]) for k, (a, b) in enumerate(pieces)]

    def back(c):
        at = pl.ds(c * size, size)
        return pltpu.make_async_copy(grad_v.at[at], grad.at[at], sems.at[3, c])

    for c in range(CHUNKS):
        for copy in copies(c):
            copy.start()
    for c in range(CHUNKS):
        for copy in copies(c):
            copy.wait()
        span = range(c * size, (c + 1) * size)
        out = [mul(twice(gram_v[t]), quad(*split(users_v[t]))) for t in span]
        for t, x in zip(span, out):
            grad_v[t] = x - moved_v[t]
        back(c).start()
    for c in range(CHUNKS):
        back(c).wait()


def user_grad_call(users, gram, moved):
    any_space = pl.BlockSpec(memory_space=pl.ANY)
    return pl.pallas_call(
        user_grad_kernel,
        in_specs=[any_space] * 3,
        out_specs=any_space,
        out_shape=jax.ShapeDtypeStruct(users.shape, F32),
        scratch_shapes=[
            pltpu.VMEM(users.shape, F32),
            pltpu.VMEM(gram.shape, BF),
            pltpu.VMEM(users.shape, F32),
            pltpu.VMEM(users.shape, F32),
            pltpu.SemaphoreType.DMA((4, CHUNKS)),
        ],
        compiler_params=pltpu.CompilerParams(vmem_limit_bytes=60 * 2**20),
        cost_estimate=pl.CostEstimate(flops=10**9, bytes_accessed=2 * 10**7, transcendentals=0),
        name="user_grad",
    )(users, gram, moved)


def tile_kernel(group, slots_user, slots_item, steps, count, users, right, cores, values, mixed,
                grad, sums, left, core_t, sums_hl):
    rank, width = users.shape[1], users.shape[2]
    block = pl.program_id(0)

    @pl.when(block == 0)
    def _():
        def prep(ks):
            x = [split(users[k]) for k in ks]
            h = [mul_t(cat(y, 1), pairs(*y)) for y in x]
            h = [cat(split(y[:, :rank] + y[:, rank:]), 1) for y in h]
            for k, y, z in zip(ks, x, h):
                left[k] = cat([-y[0], -y[1], z], 1)
                grad[k, :rank] = jnp.zeros((rank, width), F32)
        in_groups(users.shape[0], PREP, prep)
        for k in range(cores.shape[0]):
            core_t[k] = cat(split(cores[k].T), 1)
        sums_hl[...] = jnp.zeros_like(sums_hl)

    @pl.when(block * group < count[0])
    def _():
        span = range(group)
        tile = [block * group + t for t in span]
        item = [slots_item[k] for k in tile]
        step = [steps[k] for k in tile]
        inner = []
        for t in span:
            x = left[slots_user[tile[t]]]
            v, m = values[t], mixed[t]
            inner.append(mul(cat([x, x[:, 2 * width:]], 1), cat([v, v, quad(m[:rank], m[rank:])], 0)))
        inner = [split(jnp.where(tile[t] < count[0], inner[t], 0.0)) for t in span]
        grad_v = [mul(twice(core_t[step[t]]), quad(*inner[t])) for t in span]
        dcore = []
        for t in span:
            a = mul_t(cat(inner[t], 0), right[item[t]])
            dcore.append(a[:rank] + a[rank:])
        for t in span:
            grad[item[t], :rank] += grad_v[t]
            sums_hl[step[t]] += dcore[t]

    @pl.when(block == pl.num_programs(0) - 1)
    def _():
        for k in range(sums.shape[0]):
            a = sums_hl[k]
            sums[k] = a[:, :rank] + a[:, rank:]


def tile_call(slots_user, slots_item, steps, count, users, right, cores, values, mixed, extra, group=32):
    slots, width = values.shape[:2]
    held, rank = users.shape[:2]
    return pl.pallas_call(
        functools.partial(tile_kernel, group),
        grid_spec=pltpu.PrefetchScalarGridSpec(
            num_scalar_prefetch=4,
            grid=(slots // group,),
            in_specs=[whole(users.shape), whole(right.shape), whole(cores.shape),
                      pl.BlockSpec((group, width, width), live_block(group)),
                      pl.BlockSpec((group, 2 * rank, width), live_block(group))],
            out_specs=[whole((held, rank + extra, width)), whole(cores.shape)],
            scratch_shapes=[pltpu.VMEM((held, rank, 2 * width + 2 * rank), BF),
                            pltpu.VMEM((cores.shape[0], rank, 2 * rank), BF),
                            pltpu.VMEM((cores.shape[0], rank, 2 * rank), F32)],
        ),
        out_shape=[jax.ShapeDtypeStruct((held, rank + extra, width), F32),
                   jax.ShapeDtypeStruct(cores.shape, F32)],
        compiler_params=params(),
        cost_estimate=pl.CostEstimate(flops=3 * 10**10, bytes_accessed=5 * 10**7, transcendentals=0),
        name="tile_side",
    )(slots_user, slots_item, steps, count, users, right, cores, values, mixed)

def ask_kernel(held, table, out, buffer, sems):
    size = buffer.shape[0] // CHUNKS

    def send(c):
        at = pl.ds(c * size, size)
        return pltpu.make_async_copy(buffer.at[at], out.at[at], sems.at[c])

    for c in range(CHUNKS):
        for t in range(c * size, (c + 1) * size, 4):
            new = [table[held[t + k]] for k in range(4)]
            for k in range(4):
                buffer[t + k] = new[k]
        send(c).start()
    for c in range(CHUNKS):
        send(c).wait()


def asked(held, table):
    shape = (held.shape[0],) + table.shape[1:]
    return pl.pallas_call(
        ask_kernel,
        in_specs=[pl.BlockSpec(memory_space=pltpu.SMEM), pl.BlockSpec(memory_space=pltpu.VMEM)],
        out_specs=pl.BlockSpec(memory_space=pl.ANY),
        out_shape=jax.ShapeDtypeStruct(shape, F32),
        scratch_shapes=[pltpu.VMEM(shape, F32), pltpu.SemaphoreType.DMA((CHUNKS,))],
        compiler_params=pltpu.CompilerParams(vmem_limit_bytes=60 * 2**20),
        cost_estimate=pl.CostEstimate(flops=0, bytes_accessed=10**7, transcendentals=0),
        name="asked",
    )(held, table)


ADDERS = 4


def owner_kernel(rank, scale, held, back, out, *rest):
    adders, (back_v, sems) = rest[:ADDERS], rest[ADDERS:]
    size = back_v.shape[0] // CHUNKS

    def fetch(c):
        at = pl.ds(c * size, size)
        return pltpu.make_async_copy(back.at[at, pl.ds(0, rank)], back_v.at[at], sems.at[c])

    for c in range(CHUNKS):
        fetch(c).start()
    for a in adders:
        a[...] = jnp.zeros_like(a)
    for c in range(CHUNKS):
        fetch(c).wait()
        for t in range(c * size, (c + 1) * size, ADDERS):
            at = [held[t + k] for k in range(ADDERS)]
            new = [adders[k][at[k]] + back_v[t + k] for k in range(ADDERS)]
            for k in range(ADDERS):
                adders[k][at[k]] = new[k]
    total = adders[0][...]
    for a in adders[1:]:
        total = total + a[...]
    out[...] = scale * total


def owner_sum(held, back, blocks_own, rank, scale):
    total, rows, width = back.shape
    return pl.pallas_call(
        functools.partial(owner_kernel, rank, scale),
        in_specs=[pl.BlockSpec(memory_space=pltpu.SMEM), pl.BlockSpec(memory_space=pl.ANY)],
        out_specs=pl.BlockSpec(memory_space=pltpu.VMEM),
        out_shape=jax.ShapeDtypeStruct((blocks_own, rank, width), F32),
        scratch_shapes=[pltpu.VMEM((blocks_own, rank, width), F32) for _ in range(ADDERS)]
        + [pltpu.VMEM((total, rank, width), F32), pltpu.SemaphoreType.DMA((CHUNKS,))],
        compiler_params=pltpu.CompilerParams(vmem_limit_bytes=60 * 2**20),
        cost_estimate=pl.CostEstimate(flops=10**7, bytes_accessed=10**7, transcendentals=0),
        name="owner_sum",
    )(held, back)


def core_kernel(odd, mine, other, core):
    half = mine.shape[2] // 2
    rows = 2 * mine.shape[1]

    def step(ks):
        a = [mine[k] for k in ks]
        b = [other[k] for k in ks]
        new = []
        for x, y in zip(a, b):
            new.append((jnp.where(odd[0] == 0, x, y), jnp.where(odd[0] == 0, y, x)))
        new = [[cat([x[:, :half], x[:, half:]], 0) for x in pair] for pair in new]
        for k, (x, y) in zip(ks, new):
            core[k, :rows] = x
            core[k, rows:] = y

    for g in range(0, mine.shape[0], PREP):
        step(range(g, g + PREP))


def core_unpack(odd, mine, other):
    owners, rows, width = mine.shape
    return pl.pallas_call(
        core_kernel,
        in_specs=[pl.BlockSpec(memory_space=pltpu.SMEM)] + [pl.BlockSpec(memory_space=pltpu.VMEM)] * 2,
        out_specs=pl.BlockSpec(memory_space=pltpu.VMEM),
        out_shape=jax.ShapeDtypeStruct((owners, 4 * rows, width // 2), F32),
        compiler_params=pltpu.CompilerParams(vmem_limit_bytes=60 * 2**20),
        cost_estimate=pl.CostEstimate(flops=10**6, bytes_accessed=3 * 10**6, transcendentals=0),
        name="core_unpack",
    )(odd, mine, other)


def to_all(x):
    return lax.all_to_all(x, AXES, split_axis=0, concat_axis=0, tiled=True)


def from_row(x, distance):
    count = lax.axis_size("rows")
    return lax.ppermute(x, "rows", [(r, r ^ distance) for r in range(count)])


def shards(
    tile_values,
    tile_users,
    tile_items,
    tile_steps,
    tile_count,
    users_ask,
    items_ask,
    user_factor,
    item_factor,
    time_factor,
    core,
):
    rank = user_factor.shape[1]
    width = user_factor.shape[2]
    blocks_own = user_factor.shape[0]
    step_count = time_factor.shape[0]
    count_tm = lax.axis_size("tm")
    count_rows = lax.axis_size("rows")
    owners = count_tm * count_rows
    part = rank * rank // owners
    sum_rows = step_count * part // width
    core_rows = part * rank // width // 2
    asks = to_all(cat([users_ask, items_ask], 1))
    held_user, held_item = asks[:, 0], asks[:, 1]
    items = to_all(asked(held_item, item_factor))
    found_user = asked(held_user, user_factor)
    step_cores = jnp.einsum("pqr,sr->spq", core, time_factor, precision=HIGH)
    found_user, items, step_cores = lax.optimization_barrier((found_user, items, step_cores))
    users = to_all(found_user)
    gram, moved, mixed, right = item_call(
        tile_users, tile_items, tile_steps, tile_count, items, step_cores, tile_values
    )
    slot_left = user_grad_call(users, gram, moved)
    users, slot_left = lax.optimization_barrier((users, slot_left))
    back_left = to_all(slot_left)
    slot_right, step_sums = tile_call(
        tile_users, tile_items, tile_steps, tile_count, users, right, step_cores, tile_values, mixed, core_rows
    )
    parts = step_sums.reshape(step_count, owners, part).transpose(1, 0, 2).reshape(owners, sum_rows, width)
    row = lax.dynamic_slice_in_dim(time_factor, lax.axis_index("rows"), 1, 0)
    row = jnp.pad(row, ((0, 0), (0, width - rank)))
    blank = jnp.zeros((-(sum_rows + 1) % 4, width), F32)
    shared = cat([row, blank], 0)
    sent = cat([parts, jnp.broadcast_to(shared[None], (owners,) + shared.shape)], 1)
    sent, back_left = lax.optimization_barrier((sent, back_left))
    got = to_all(sent)
    some = got[:, :sum_rows].reshape(count_tm, count_rows, step_count, part)
    some = jnp.sum(some, axis=1).reshape(count_tm * step_count, part)
    every_time = got[:, sum_rows, :rank]
    own = core_scale * jnp.einsum("sk,sr->kr", some, every_time, precision=HIGH)
    own = own.reshape(2, 2, core_rows, rank).transpose(0, 2, 1, 3).reshape(1, 2, core_rows, width)
    own = jnp.broadcast_to(own, (owners // 2, 2, core_rows, width)).reshape(owners, core_rows, width)
    slot_right = slot_right.at[:, rank:].set(own)
    back_right = to_all(slot_right)
    grad_users = owner_sum(held_user, back_left, blocks_own, rank, user_scale)
    step_sums, grad_users = lax.optimization_barrier((step_sums, grad_users))
    own_time = jnp.einsum("spq,pqr->sr", step_sums, core, precision=HIGH)
    for distance in [1 << k for k in range(count_rows.bit_length() - 1)]:
        own_time = own_time + from_row(own_time, distance)
    grad_time = time_scale * own_time
    back_right, grad_users, grad_time = lax.optimization_barrier((back_right, grad_users, grad_time))
    mine = back_right[:, rank:]
    other = from_row(mine, 1)
    grad_items = owner_sum(held_item, back_right, blocks_own, rank, user_scale)
    odd = (lax.axis_index("rows") % 2).astype(jnp.int32).reshape(1)
    grad_core = core_unpack(odd, mine, other).reshape(rank, rank, rank)
    return (grad_users, grad_items, grad_time, grad_core)


def solution(mesh):
    in_specs = (
        P(AXES, None, None),
        P(AXES),
        P(AXES),
        P(AXES),
        P(AXES),
        P(AXES, None),
        P(AXES, None),
        P(AXES, None, None),
        P(AXES, None, None),
        P("tm", None),
        P(),
    )
    out_specs = (P(AXES, None, None), P(AXES, None, None), P("tm", None), P())
    return jax.shard_map(shards, mesh=mesh, in_specs=in_specs, out_specs=out_specs, check_vma=False)
```

```python
import functools

import jax
import jax.numpy as jnp
from jax import lax
from jax.experimental import pallas as pl
from jax.experimental.pallas import tpu as pltpu
from jax.sharding import PartitionSpec as P

HIGH = lax.Precision.HIGHEST
user_scale = 0.125
time_scale = 1.0 / 2048.0
core_scale = 1.0 / 4096.0

BF = jnp.bfloat16
F32 = jnp.float32
AXES = ("tm", "rows")
cat = jnp.concatenate
PREP = 8


def split(x):
    hi = x.astype(BF)
    lo = (x - hi.astype(F32)).astype(BF)
    return hi, lo


def mul(a, b):
    return lax.dot_general(a, b, (((1,), (0,)), ((), ())), preferred_element_type=F32)


def mul_t(a, b):
    return lax.dot_general(a, b, (((1,), (1,)), ((), ())), preferred_element_type=F32)


def twice(x):
    return cat([x, x], 1)


def quad(hi, lo):
    return cat([hi, hi, lo, lo], 0)


def pairs(hi, lo):
    return cat([twice(hi), twice(lo)], 0)


def whole(shape):
    return pl.BlockSpec(shape, lambda b, *_: (0,) * len(shape), pipeline_mode=pl.Buffered(1))


def live_block(group):
    def at(b, *scalars):
        last = jnp.maximum((scalars[-1][0] + group - 1) // group - 1, 0)
        return (jnp.minimum(b, last), 0, 0)
    return at


def params():
    return pltpu.CompilerParams(vmem_limit_bytes=60 * 2**20, dimension_semantics=("arbitrary",))


def in_groups(total, size, step):
    def one(g, carry):
        step([g * size + t for t in range(size)])
        return carry
    lax.fori_loop(0, total // size, one, 0)


def item_kernel(group, slots_user, slots_item, steps, count, items, cores, values,
                gram, moved, mixed_out, right, core_hl, gram_sum):
    rank, width = items.shape[1], items.shape[2]
    block = pl.program_id(0)

    @pl.when(block == 0)
    def _():
        def prep(ks):
            out = [cat(split(items[k]), 0) for k in ks]
            for k, x in zip(ks, out):
                right[k] = x
            for k in ks:
                gram_sum[k] = jnp.zeros_like(gram_sum[k])
                moved[k] = jnp.zeros_like(moved[k])
        in_groups(items.shape[0], PREP, prep)
        for k in range(cores.shape[0]):
            core_hl[k] = cat(split(cores[k]), 1)

    @pl.when(block * group < count[0])
    def _():
        span = range(group)
        tile = [block * group + t for t in span]
        user = [slots_user[k] for k in tile]
        mixed = []
        for t in span:
            r = right[slots_item[tile[t]]]
            mixed.append(mul(twice(core_hl[steps[tile[t]]]), quad(r[:rank], r[rank:])))
        mixed = [split(jnp.where(tile[t] < count[0], mixed[t], 0.0)) for t in span]
        both = []
        for t in span:
            v = values[t]
            both.append(mul_t(cat(mixed[t], 1), cat([twice(v), pairs(*mixed[t])], 0)))
        for t in span:
            mixed_out[t] = cat(mixed[t], 0)
        for t in span:
            moved[user[t]] += both[t][:, :width]
            gram_sum[user[t]] += both[t][:, width:]

    @pl.when(block == pl.num_programs(0) - 1)
    def _():
        def finish(ks):
            out = [gram_sum[k] for k in ks]
            out = [cat(split(x[:, :rank] + x[:, rank:]), 1) for x in out]
            for k, x in zip(ks, out):
                gram[k] = x
        in_groups(gram.shape[0], PREP, finish)


def item_call(slots_user, slots_item, steps, count, items, cores, values, group=32):
    slots, width = values.shape[:2]
    held, rank = items.shape[:2]
    return pl.pallas_call(
        functools.partial(item_kernel, group),
        grid_spec=pltpu.PrefetchScalarGridSpec(
            num_scalar_prefetch=4,
            grid=(slots // group,),
            in_specs=[whole(items.shape), whole(cores.shape),
                      pl.BlockSpec((group, width, width), live_block(group))],
            out_specs=[whole((held, rank, 2 * rank)), whole((held, rank, width)),
                       pl.BlockSpec((group, 2 * rank, width), live_block(group)),
                       whole((held, 2 * rank, width))],
            scratch_shapes=[pltpu.VMEM((cores.shape[0], rank, 2 * rank), BF),
                            pltpu.VMEM((held, rank, 2 * rank), F32)],
        ),
        out_shape=[jax.ShapeDtypeStruct((held, rank, 2 * rank), BF),
                   jax.ShapeDtypeStruct((held, rank, width), F32),
                   jax.ShapeDtypeStruct((slots, 2 * rank, width), BF),
                   jax.ShapeDtypeStruct((held, 2 * rank, width), BF)],
        compiler_params=params(),
        cost_estimate=pl.CostEstimate(flops=2 * 10**10, bytes_accessed=5 * 10**7, transcendentals=0),
        name="item_side",
    )(slots_user, slots_item, steps, count, items, cores, values)


CHUNKS = 8


def user_grad_kernel(users, gram, moved, grad, users_v, gram_v, moved_v, grad_v, sems):
    size = users_v.shape[0] // CHUNKS

    def copies(c):
        at = pl.ds(c * size, size)
        pieces = ((users, users_v), (gram, gram_v), (moved, moved_v))
        return [pltpu.make_async_copy(a.at[at], b.at[at], sems.at[k, c]) for k, (a, b) in enumerate(pieces)]

    def back(c):
        at = pl.ds(c * size, size)
        return pltpu.make_async_copy(grad_v.at[at], grad.at[at], sems.at[3, c])

    for c in range(CHUNKS):
        for copy in copies(c):
            copy.start()
    for c in range(CHUNKS):
        for copy in copies(c):
            copy.wait()
        span = range(c * size, (c + 1) * size)
        out = [mul(twice(gram_v[t]), quad(*split(users_v[t]))) for t in span]
        for t, x in zip(span, out):
            grad_v[t] = x - moved_v[t]
        back(c).start()
    for c in range(CHUNKS):
        back(c).wait()


def user_grad_call(users, gram, moved):
    any_space = pl.BlockSpec(memory_space=pl.ANY)
    return pl.pallas_call(
        user_grad_kernel,
        in_specs=[any_space] * 3,
        out_specs=any_space,
        out_shape=jax.ShapeDtypeStruct(users.shape, F32),
        scratch_shapes=[
            pltpu.VMEM(users.shape, F32),
            pltpu.VMEM(gram.shape, BF),
            pltpu.VMEM(users.shape, F32),
            pltpu.VMEM(users.shape, F32),
            pltpu.SemaphoreType.DMA((4, CHUNKS)),
        ],
        compiler_params=pltpu.CompilerParams(vmem_limit_bytes=60 * 2**20),
        cost_estimate=pl.CostEstimate(flops=10**9, bytes_accessed=2 * 10**7, transcendentals=0),
        name="user_grad",
    )(users, gram, moved)


def tile_kernel(group, slots_user, slots_item, steps, count, users, right, cores, values, mixed,
                grad, sums, left, core_t, sums_hl):
    rank, width = users.shape[1], users.shape[2]
    block = pl.program_id(0)

    @pl.when(block == 0)
    def _():
        def prep(ks):
            x = [split(users[k]) for k in ks]
            h = [mul_t(cat(y, 1), pairs(*y)) for y in x]
            h = [cat(split(y[:, :rank] + y[:, rank:]), 1) for y in h]
            for k, y, z in zip(ks, x, h):
                left[k] = cat([-y[0], -y[1], z], 1)
                grad[k, :rank] = jnp.zeros((rank, width), F32)
        in_groups(users.shape[0], PREP, prep)
        for k in range(cores.shape[0]):
            core_t[k] = cat(split(cores[k].T), 1)
        sums_hl[...] = jnp.zeros_like(sums_hl)

    @pl.when(block * group < count[0])
    def _():
        span = range(group)
        tile = [block * group + t for t in span]
        item = [slots_item[k] for k in tile]
        step = [steps[k] for k in tile]
        inner = []
        for t in span:
            x = left[slots_user[tile[t]]]
            v, m = values[t], mixed[t]
            inner.append(mul(cat([x, x[:, 2 * width:]], 1), cat([v, v, quad(m[:rank], m[rank:])], 0)))
        inner = [split(jnp.where(tile[t] < count[0], inner[t], 0.0)) for t in span]
        grad_v = [mul(twice(core_t[step[t]]), quad(*inner[t])) for t in span]
        dcore = []
        for t in span:
            a = mul_t(cat(inner[t], 0), right[item[t]])
            dcore.append(a[:rank] + a[rank:])
        for t in span:
            grad[item[t], :rank] += grad_v[t]
            sums_hl[step[t]] += dcore[t]

    @pl.when(block == pl.num_programs(0) - 1)
    def _():
        for k in range(sums.shape[0]):
            a = sums_hl[k]
            sums[k] = a[:, :rank] + a[:, rank:]


def tile_call(slots_user, slots_item, steps, count, users, right, cores, values, mixed, extra, group=32):
    slots, width = values.shape[:2]
    held, rank = users.shape[:2]
    return pl.pallas_call(
        functools.partial(tile_kernel, group),
        grid_spec=pltpu.PrefetchScalarGridSpec(
            num_scalar_prefetch=4,
            grid=(slots // group,),
            in_specs=[whole(users.shape), whole(right.shape), whole(cores.shape),
                      pl.BlockSpec((group, width, width), live_block(group)),
                      pl.BlockSpec((group, 2 * rank, width), live_block(group))],
            out_specs=[whole((held, rank + extra, width)), whole(cores.shape)],
            scratch_shapes=[pltpu.VMEM((held, rank, 2 * width + 2 * rank), BF),
                            pltpu.VMEM((cores.shape[0], rank, 2 * rank), BF),
                            pltpu.VMEM((cores.shape[0], rank, 2 * rank), F32)],
        ),
        out_shape=[jax.ShapeDtypeStruct((held, rank + extra, width), F32),
                   jax.ShapeDtypeStruct(cores.shape, F32)],
        compiler_params=params(),
        cost_estimate=pl.CostEstimate(flops=3 * 10**10, bytes_accessed=5 * 10**7, transcendentals=0),
        name="tile_side",
    )(slots_user, slots_item, steps, count, users, right, cores, values, mixed)

def ask_kernel(held, table, out, buffer, sems):
    size = buffer.shape[0] // CHUNKS

    def send(c):
        at = pl.ds(c * size, size)
        return pltpu.make_async_copy(buffer.at[at], out.at[at], sems.at[c])

    for c in range(CHUNKS):
        for t in range(c * size, (c + 1) * size, 4):
            new = [table[held[t + k]] for k in range(4)]
            for k in range(4):
                buffer[t + k] = new[k]
        send(c).start()
    for c in range(CHUNKS):
        send(c).wait()


def asked(held, table):
    shape = (held.shape[0],) + table.shape[1:]
    return pl.pallas_call(
        ask_kernel,
        in_specs=[pl.BlockSpec(memory_space=pltpu.SMEM), pl.BlockSpec(memory_space=pltpu.VMEM)],
        out_specs=pl.BlockSpec(memory_space=pl.ANY),
        out_shape=jax.ShapeDtypeStruct(shape, F32),
        scratch_shapes=[pltpu.VMEM(shape, F32), pltpu.SemaphoreType.DMA((CHUNKS,))],
        compiler_params=pltpu.CompilerParams(vmem_limit_bytes=60 * 2**20),
        cost_estimate=pl.CostEstimate(flops=0, bytes_accessed=10**7, transcendentals=0),
        name="asked",
    )(held, table)


ADDERS = 4


def owner_kernel(rank, scale, held, back, out, *rest):
    adders, (back_v, sems) = rest[:ADDERS], rest[ADDERS:]
    size = back_v.shape[0] // CHUNKS

    def fetch(c):
        at = pl.ds(c * size, size)
        return pltpu.make_async_copy(back.at[at, pl.ds(0, rank)], back_v.at[at], sems.at[c])

    for c in range(CHUNKS):
        fetch(c).start()
    for a in adders:
        a[...] = jnp.zeros_like(a)
    for c in range(CHUNKS):
        fetch(c).wait()
        for t in range(c * size, (c + 1) * size, ADDERS):
            at = [held[t + k] for k in range(ADDERS)]
            new = [adders[k][at[k]] + back_v[t + k] for k in range(ADDERS)]
            for k in range(ADDERS):
                adders[k][at[k]] = new[k]
    total = adders[0][...]
    for a in adders[1:]:
        total = total + a[...]
    out[...] = scale * total


def owner_sum(held, back, blocks_own, rank, scale):
    total, rows, width = back.shape
    return pl.pallas_call(
        functools.partial(owner_kernel, rank, scale),
        in_specs=[pl.BlockSpec(memory_space=pltpu.SMEM), pl.BlockSpec(memory_space=pl.ANY)],
        out_specs=pl.BlockSpec(memory_space=pltpu.VMEM),
        out_shape=jax.ShapeDtypeStruct((blocks_own, rank, width), F32),
        scratch_shapes=[pltpu.VMEM((blocks_own, rank, width), F32) for _ in range(ADDERS)]
        + [pltpu.VMEM((total, rank, width), F32), pltpu.SemaphoreType.DMA((CHUNKS,))],
        compiler_params=pltpu.CompilerParams(vmem_limit_bytes=60 * 2**20),
        cost_estimate=pl.CostEstimate(flops=10**7, bytes_accessed=10**7, transcendentals=0),
        name="owner_sum",
    )(held, back)


def owner_core_kernel(rank, scale, held, odd, back, mine, other, out, core, *rest):
    adders, (back_v, core_v, sems, core_sem) = rest[:ADDERS], rest[ADDERS:]
    size = back_v.shape[0] // CHUNKS
    half, rows = mine.shape[2] // 2, 2 * mine.shape[1]

    def fetch(c):
        at = pl.ds(c * size, size)
        return pltpu.make_async_copy(back.at[at, pl.ds(0, rank)], back_v.at[at], sems.at[c])

    for c in range(CHUNKS):
        fetch(c).start()
    for a in adders:
        a[...] = jnp.zeros_like(a)
    for g in range(0, mine.shape[0], PREP):
        span = range(g, g + PREP)
        pair = [(mine[k], other[k]) for k in span]
        pair = [(jnp.where(odd[0] == 0, x, y), jnp.where(odd[0] == 0, y, x)) for x, y in pair]
        pair = [[cat([x[:, :half], x[:, half:]], 0) for x in both] for both in pair]
        for k, (x, y) in zip(span, pair):
            core_v[k, :rows] = x
            core_v[k, rows:] = y
    leave = pltpu.make_async_copy(core_v, core, core_sem)
    leave.start()
    for c in range(CHUNKS):
        fetch(c).wait()
        for t in range(c * size, (c + 1) * size, ADDERS):
            at = [held[t + k] for k in range(ADDERS)]
            new = [adders[k][at[k]] + back_v[t + k] for k in range(ADDERS)]
            for k in range(ADDERS):
                adders[k][at[k]] = new[k]
    total = adders[0][...]
    for a in adders[1:]:
        total = total + a[...]
    out[...] = scale * total
    leave.wait()


def owner_core_sum(held, odd, back, mine, other, blocks_own, rank, scale):
    total, rows, width = back.shape
    core_shape = (total, 4 * mine.shape[1], width // 2)
    small, local = pl.BlockSpec(memory_space=pltpu.SMEM), pl.BlockSpec(memory_space=pltpu.VMEM)
    far = pl.BlockSpec(memory_space=pltpu.HBM)
    return pl.pallas_call(
        functools.partial(owner_core_kernel, rank, scale),
        in_specs=[small, small, far, local, local],
        out_specs=[local, far],
        out_shape=[
            jax.ShapeDtypeStruct((blocks_own, rank, width), F32),
            jax.ShapeDtypeStruct(core_shape, F32),
        ],
        scratch_shapes=[pltpu.VMEM((blocks_own, rank, width), F32) for _ in range(ADDERS)]
        + [
            pltpu.VMEM((total, rank, width), F32),
            pltpu.VMEM(core_shape, F32),
            pltpu.SemaphoreType.DMA((CHUNKS,)),
            pltpu.SemaphoreType.DMA,
        ],
        compiler_params=pltpu.CompilerParams(vmem_limit_bytes=40 * 2**20),
        cost_estimate=pl.CostEstimate(flops=10**7, bytes_accessed=10**7, transcendentals=0),
        name="owner_core_sum",
    )(held, odd, back, mine, other)


def to_all(x):
    return lax.all_to_all(x, AXES, split_axis=0, concat_axis=0, tiled=True)


def from_row(x, distance):
    count = lax.axis_size("rows")
    return lax.ppermute(x, "rows", [(r, r ^ distance) for r in range(count)])


def shards(
    tile_values,
    tile_users,
    tile_items,
    tile_steps,
    tile_count,
    users_ask,
    items_ask,
    user_factor,
    item_factor,
    time_factor,
    core,
):
    rank = user_factor.shape[1]
    width = user_factor.shape[2]
    blocks_own = user_factor.shape[0]
    step_count = time_factor.shape[0]
    count_tm = lax.axis_size("tm")
    count_rows = lax.axis_size("rows")
    owners = count_tm * count_rows
    part = rank * rank // owners
    sum_rows = step_count * part // width
    core_rows = part * rank // width // 2
    asks = to_all(cat([users_ask, items_ask], 1))
    held_user, held_item = asks[:, 0], asks[:, 1]
    items = to_all(asked(held_item, item_factor))
    found_user = asked(held_user, user_factor)
    step_cores = jnp.einsum("pqr,sr->spq", core, time_factor, precision=HIGH)
    found_user, items, step_cores = lax.optimization_barrier((found_user, items, step_cores))
    users = to_all(found_user)
    gram, moved, mixed, right = item_call(
        tile_users, tile_items, tile_steps, tile_count, items, step_cores, tile_values
    )
    slot_left = user_grad_call(users, gram, moved)
    users, slot_left = lax.optimization_barrier((users, slot_left))
    back_left = to_all(slot_left)
    slot_right, step_sums = tile_call(
        tile_users, tile_items, tile_steps, tile_count, users, right, step_cores, tile_values, mixed, core_rows
    )
    parts = step_sums.reshape(step_count, owners, part).transpose(1, 0, 2).reshape(owners, sum_rows, width)
    row = lax.dynamic_slice_in_dim(time_factor, lax.axis_index("rows"), 1, 0)
    row = jnp.pad(row, ((0, 0), (0, width - rank)))
    blank = jnp.zeros((-(sum_rows + 1) % 4, width), F32)
    shared = cat([row, blank], 0)
    sent = cat([parts, jnp.broadcast_to(shared[None], (owners,) + shared.shape)], 1)
    sent, back_left = lax.optimization_barrier((sent, back_left))
    got = to_all(sent)
    some = got[:, :sum_rows].reshape(count_tm, count_rows, step_count, part)
    some = jnp.sum(some, axis=1).reshape(count_tm * step_count, part)
    every_time = got[:, sum_rows, :rank]
    own = core_scale * jnp.einsum("sk,sr->kr", some, every_time, precision=HIGH)
    own = own.reshape(2, 2, core_rows, rank).transpose(0, 2, 1, 3).reshape(1, 2, core_rows, width)
    own = jnp.broadcast_to(own, (owners // 2, 2, core_rows, width)).reshape(owners, core_rows, width)
    slot_right = slot_right.at[:, rank:].set(own)
    back_right = to_all(slot_right)
    grad_users = owner_sum(held_user, back_left, blocks_own, rank, user_scale)
    step_sums, grad_users = lax.optimization_barrier((step_sums, grad_users))
    own_time = jnp.einsum("spq,pqr->sr", step_sums, core, precision=HIGH)
    for distance in [1 << k for k in range(count_rows.bit_length() - 1)]:
        own_time = own_time + from_row(own_time, distance)
    grad_time = time_scale * own_time
    back_right, grad_users, grad_time = lax.optimization_barrier((back_right, grad_users, grad_time))
    mine = back_right[:, rank:]
    other = from_row(mine, 1)
    odd = (lax.axis_index("rows") % 2).astype(jnp.int32).reshape(1)
    grad_items, grad_core = owner_core_sum(
        held_item, odd, back_right, mine, other, blocks_own, rank, user_scale
    )
    grad_core = grad_core.reshape(rank, rank, rank)
    return (grad_users, grad_items, grad_time, grad_core)


def solution(mesh):
    in_specs = (
        P(AXES, None, None),
        P(AXES),
        P(AXES),
        P(AXES),
        P(AXES),
        P(AXES, None),
        P(AXES, None),
        P(AXES, None, None),
        P(AXES, None, None),
        P("tm", None),
        P(),
    )
    out_specs = (P(AXES, None, None), P(AXES, None, None), P("tm", None), P())
    return jax.shard_map(shards, mesh=mesh, in_specs=in_specs, out_specs=out_specs, check_vma=False)
```
